32 devices in a mesh: grp: 2 (over y), dom: 4 (over z), sub: 2 (over x), feat: 2 (over core).
Axes of the slice: x: 2, y: 2, z: 4, core: 2. Of those that a mesh axis runs over, the one named last changes fastest.
Arguments:
- features: bfloat16 [32768, 256], P(('grp', 'dom', 'sub', 'feat')), parts along dimension 0, may hold values from -6 to 6
- labels: int32 [32768], P(('grp', 'dom', 'sub', 'feat')), parts along dimension 0, may hold values from 0 to 127
- local_index: int32 [256, 4], P(('grp', 'dom', 'sub', 'feat')), parts along dimension 0, may hold values from 0 to 7
- local_values: bfloat16 [256, 4, 128, 128], P(('grp', 'dom', 'sub', 'feat')), parts along dimension 0, may hold values from -0.25 to 0.25
- cross_src: int32 [32, 3, 4], P(('grp', 'dom', 'sub', 'feat')), parts along dimension 0, may hold values from 0 to 7, as said below
- cross_dst: int32 [32, 3, 4], P(('grp', 'dom', 'sub', 'feat')), parts along dimension 0, may hold values from 0 to 7
- cross_count: int32 [32, 3], P(('grp', 'dom', 'sub', 'feat')), parts along dimension 0, may hold values from 1 to 4, as said below
- cross_values: bfloat16 [32, 3, 4, 128, 128], P(('grp', 'dom', 'sub', 'feat')), parts along dimension 0, may hold values from -0.25 to 0.25
- w1_self: bfloat16 [256, 256], replicated, may hold values from -0.375 to 0.375
- w1_near: bfloat16 [256, 256], replicated, may hold values from -0.375 to 0.375
- bias_one: float32 [256], replicated, may hold values from -3 to 3
- w2_self: bfloat16 [256, 128], replicated, may hold values from -0.375 to 0.375
- w2_near: bfloat16 [256, 128], replicated, may hold values from -0.375 to 0.375
- bias_two: float32 [128], replicated, may hold values from -3 to 3
Outputs:
- logits: bfloat16 [32768, 128], P(('grp', 'dom', 'sub', 'feat')), parts along dimension 0
- hidden_grad: bfloat16 [32768, 256], P(('grp', 'dom', 'sub', 'feat')), parts along dimension 0
- grad_w1_self: float32 [512, 256], P('grp'), parts along dimension 0
- grad_w1_near: float32 [512, 256], P('grp'), parts along dimension 0
- grad_bias_one: float32 [512], P('grp'), parts along dimension 0
- grad_w2_self: float32 [512, 128], P('grp'), parts along dimension 0
- grad_w2_near: float32 [512, 128], P('grp'), parts along dimension 0
- grad_bias_two: float32 [256], P('grp'), parts along dimension 0
The draws below stay inside these ranges and needn't reach their ends.
There are 2 independent parts, one for each index of `grp`. The reference program is written for one: setup_inputs(seed, part) draws one part's arguments, and reference() takes and returns one part's arrays. A program takes and returns all parts, laid end to end along the dimension named above; an argument that names none is the same for every part. Nothing has to cross between parts.
Inputs may be any that keep to these rules, and one draw needn't show every extreme that they name: `cross_src`: for one partition and one colour round the 4 entries are distinct tiles of the partner. `cross_count`: slots at or beyond the count are unused; the count 4 occurs in every draw.
All inputs are finite; a program needn't handle non-finite values.
Results may differ from the reference program's by a relative error of at most 0.0062.
Values may be sent and summed in bfloat16 or wider, within the bound.
No kernel may reach another device: no remote copies, remote signals or barrier semaphores. Data moves between devices by JAX's collectives and lax.ppermute only.
A program may use at most 64 MiB of HBM per device.

```python
import jax
import jax.numpy as jnp
from jax import lax

F = 256
H = 256
C = 128
TILE = 128
ROW_TILES = 8
KL = 4
MAXB = 4
ROUNDS = 3
DEVS = 16
NODES = 16384
TILES_ALL = 128


def draw_cross_src(key, part):
    key = jax.random.fold_in(key, 7)
    ordered = jnp.broadcast_to(jnp.arange(ROW_TILES, dtype=jnp.int32), (DEVS * ROUNDS, ROW_TILES))
    shuffled = jax.random.permutation(key, ordered, axis=1, independent=True)
    return shuffled[:, :MAXB].reshape(DEVS, ROUNDS, MAXB).astype(jnp.int32)


def draw_cross_count(key, part):
    key = jax.random.fold_in(key, 11)
    random_counts = jax.random.randint(key, (DEVS, ROUNDS), 1, MAXB + 1, dtype=jnp.int32)
    diagonal_ids = jnp.arange(DEVS, dtype=jnp.int32)[:, None] + jnp.arange(ROUNDS, dtype=jnp.int32)[None, :]
    return jnp.where(diagonal_ids % 3 == 0, MAXB, random_counts).astype(jnp.int32)


def with_ends(result, rng, low, largest):
    index_at = [jax.random.randint(jax.random.fold_in(rng, axis), (), 0, length) for axis, length in enumerate(result.shape)]
    widest = result.shape.index(max(result.shape))
    beside = index_at[:widest] + [(index_at[widest] + 1) % result.shape[widest]] + index_at[widest + 1:]
    return result.at[tuple(index_at)].set(low).at[tuple(beside)].set(largest)


def spiked(drawn, own_key, source, target, blocks, factor):
    def block_of(axis_at):
        return (jnp.arange(drawn.shape[axis_at]) // (drawn.shape[axis_at] // blocks)).reshape((-1,) + (1,) * (drawn.ndim - 1 - axis_at))

    first = jax.random.permutation(own_key, blocks)[block_of(target)]
    other_side = (block_of(target) + blocks // 2) % blocks
    return jnp.where((block_of(source) == first) | (block_of(source) == other_side), factor * drawn, drawn)


def block_levels(own_key, extent, cuts, low, top_value):
    factor_of, own = 1.0, jax.random.fold_in(own_key, 6)
    for axis_at, shards_of in cuts:
        heights = jnp.exp(jax.random.uniform(jax.random.fold_in(own, axis_at), (shards_of,), jnp.float32, low / len(cuts), top_value / len(cuts)))
        factor_of = factor_of * jnp.repeat(heights, extent[axis_at] // shards_of).reshape([-1 if axis == axis_at else 1 for axis in range(len(extent))])
    return factor_of


def normal_values(rng, shape, spread, most, shards=(), held_as=jnp.bfloat16):
    result = jax.random.normal(rng, shape, jnp.float32) * spread
    if len(shards) > 0:
        result = block_levels(rng, shape, shards, -0.22, 0.18) * result
    return jnp.clip(result, min=-most, max=most).astype(held_as)


def heavy_noise(rng, dims, scale, limit, split, heavy, kind=jnp.bfloat16):
    values = scale * jax.random.normal(rng, dims, jnp.float32)
    if split:
        values = values * block_levels(rng, dims, split, -0.22, 0.18)
    return jnp.clip(spiked(values, jax.random.fold_in(rng, 3), *heavy), -limit, limit).astype(kind)


def setup_inputs(seed: int = 0, part: int = 0) -> dict:
    key_list = jax.random.split(jax.random.key(seed), 15)
    part_keys = jax.random.split(jax.random.fold_in(key_list[14], part), 15)
    return {
        "features": heavy_noise(part_keys[0], (NODES, F), 1.0, 6.0, ((0, 16),), (0, 1, 16, 2.0)),
        "labels": with_ends(jax.random.randint(part_keys[1], (NODES,), 0, C), jax.random.fold_in(part_keys[1], 1), 0, C - 1).astype(jnp.int32),
        "local_index": with_ends(jax.random.randint(part_keys[2], (TILES_ALL, KL), 0, ROW_TILES), jax.random.fold_in(part_keys[2], 1), 0, ROW_TILES - 1).astype(jnp.int32),
        "local_values": normal_values(part_keys[3], (TILES_ALL, KL, TILE, TILE), (TILE * (KL + 1)) ** -0.5, 0.25, ((0, 16),)),
        "cross_src": draw_cross_src(jax.random.fold_in(jax.random.fold_in(key_list[14], part), 71), part),
        "cross_dst": with_ends(jax.random.randint(part_keys[5], (DEVS, ROUNDS, MAXB), 0, ROW_TILES), jax.random.fold_in(part_keys[5], 1), 0, ROW_TILES - 1).astype(jnp.int32),
        "cross_count": draw_cross_count(jax.random.fold_in(jax.random.fold_in(key_list[14], part), 71), part),
        "cross_values": normal_values(part_keys[7], (DEVS, ROUNDS, MAXB, TILE, TILE), (TILE * (KL + 1)) ** -0.5, 0.25, ((0, 16),)),
        "w1_self": normal_values(key_list[8], (F, H), F ** -0.5, 0.375),
        "w1_near": normal_values(key_list[9], (F, H), F ** -0.5, 0.375),
        "bias_one": normal_values(key_list[10], (H,), 0.5, 3.0, (), jnp.float32),
        "w2_self": normal_values(key_list[11], (H, C), H ** -0.5, 0.375),
        "w2_near": normal_values(key_list[12], (H, C), H ** -0.5, 0.375),
        "bias_two": normal_values(key_list[13], (C,), 0.5, 3.0, (), jnp.float32),
    }


def silu_slope(pre_act):
    sigmoid_pre = jax.nn.sigmoid(pre_act)
    return sigmoid_pre * (1.0 + pre_act * (1.0 - sigmoid_pre))


def partner_of(colour):
    total_bits = DEVS.bit_length() - 1
    devices = jnp.arange(DEVS, dtype=jnp.int32)
    return jnp.bitwise_xor(devices, 1 << (total_bits - 1 - colour)).astype(jnp.int32)


def aggregate(blocks, local_index, local_values, cross_src, cross_dst, cross_count, cross_values):
    arrived_all = []
    for colour in range(ROUNDS):
        partner = partner_of(colour)
        arrived_all.append(blocks[partner[:, None], cross_src[:, colour, :]])
    arrived_all = jnp.stack(arrived_all, 1)
    near_index = local_index.reshape(DEVS, ROW_TILES, KL)
    near_values = local_values.reshape(DEVS, ROW_TILES, KL, TILE, TILE)
    tile_ids = jnp.arange(ROW_TILES, dtype=jnp.int32)
    slot_ids = jnp.arange(MAXB, dtype=jnp.int32)

    def one_device(packed):
        own_blocks, own_index, own_values, dest_tiles, live_count, edge_tiles, incoming = packed
        near_rows = own_blocks[own_index].astype(jnp.float32)
        summed = jnp.einsum("tkij,tkjw->tiw", own_values.astype(jnp.float32), near_rows,
                            precision=lax.Precision.HIGHEST)
        active = (slot_ids[None, :] < live_count[:, None]).astype(jnp.float32)
        products = jnp.einsum("rbij,rbjw->rbiw", edge_tiles.astype(jnp.float32), incoming.astype(jnp.float32),
                              precision=lax.Precision.HIGHEST)
        target = (dest_tiles[:, :, None] == tile_ids[None, None, :]).astype(jnp.float32) * active[:, :, None]
        return summed + jnp.einsum("rbt,rbiw->tiw", target, products, precision=lax.Precision.HIGHEST)

    return lax.map(one_device, (blocks, near_index, near_values, cross_dst, cross_count, cross_values, arrived_all))


def aggregate_back(grad_blocks, local_index, local_values, cross_src, cross_dst, cross_count, cross_values):
    near_index = local_index.reshape(DEVS, ROW_TILES, KL)
    near_values = local_values.reshape(DEVS, ROW_TILES, KL, TILE, TILE)
    tile_ids = jnp.arange(ROW_TILES, dtype=jnp.int32)
    slot_ids = jnp.arange(MAXB, dtype=jnp.int32)

    def one_device(packed):
        grad_tiles, own_index, own_values, dest_tiles, live_count, edge_tiles = packed
        local_terms = jnp.einsum("tkji,tjw->tkiw", own_values.astype(jnp.float32), grad_tiles.astype(jnp.float32),
                                 precision=lax.Precision.HIGHEST)
        owners = (own_index[:, :, None] == tile_ids[None, None, :]).astype(jnp.float32)
        summed = jnp.einsum("tks,tkiw->siw", owners, local_terms, precision=lax.Precision.HIGHEST)
        active = (slot_ids[None, :] < live_count[:, None]).astype(jnp.float32)
        sent_tiles = jnp.einsum("rbji,rbjw->rbiw", edge_tiles.astype(jnp.float32),
                                grad_tiles[dest_tiles].astype(jnp.float32), precision=lax.Precision.HIGHEST)
        sent_tiles = (sent_tiles * active[:, :, None, None]).astype(jnp.bfloat16)
        return summed, sent_tiles

    summed, sent_tiles = lax.map(one_device, (grad_blocks, near_index, near_values, cross_dst, cross_count, cross_values))
    sent_tiles = lax.optimization_barrier(sent_tiles)
    for colour in range(ROUNDS):
        partner = partner_of(colour)
        from_partner = sent_tiles[partner, colour].astype(jnp.float32)
        where_to = cross_src[partner, colour]
        placed = (where_to[:, :, None] == tile_ids[None, None, :]).astype(jnp.float32)
        summed = summed + jnp.einsum("dbt,dbiw->dtiw", placed, from_partner, precision=lax.Precision.HIGHEST)
    return summed


def reference(features, labels, local_index, local_values, cross_src, cross_dst, cross_count, cross_values,
              w1_self, w1_near, bias_one, w2_self, w2_near, bias_two):
    graph = (local_index, local_values, cross_src, cross_dst, cross_count, cross_values)
    first_agg = aggregate(features.reshape(DEVS, ROW_TILES, TILE, F), *graph).reshape(NODES, F).astype(jnp.bfloat16)
    first_pre = (jnp.dot(features, w1_self, preferred_element_type=jnp.float32)
                 + jnp.dot(first_agg, w1_near, preferred_element_type=jnp.float32) + bias_one)
    hidden = jax.nn.silu(first_pre).astype(jnp.bfloat16)
    second_agg = aggregate(hidden.reshape(DEVS, ROW_TILES, TILE, H), *graph).reshape(NODES, H).astype(jnp.bfloat16)
    second_pre = (jnp.dot(hidden, w2_self, preferred_element_type=jnp.float32)
                  + jnp.dot(second_agg, w2_near, preferred_element_type=jnp.float32) + bias_two)
    logits = second_pre.astype(jnp.bfloat16)
    target = (labels[:, None] == jnp.arange(C, dtype=jnp.int32)[None, :]).astype(jnp.float32)
    error_rows = (second_pre - target).astype(jnp.bfloat16)
    grad_w2_self = jnp.dot(hidden.T, error_rows, preferred_element_type=jnp.float32)
    grad_w2_near = jnp.dot(second_agg.T, error_rows, preferred_element_type=jnp.float32)
    grad_bias_two = jnp.sum(error_rows.astype(jnp.float32), axis=0)
    agg_grad = jnp.dot(error_rows, w2_near.T, preferred_element_type=jnp.float32).astype(jnp.bfloat16)
    self_grad = jnp.dot(error_rows, w2_self.T, preferred_element_type=jnp.float32)
    back_sum = aggregate_back(agg_grad.reshape(DEVS, ROW_TILES, TILE, H), *graph).reshape(NODES, H)
    full_grad = self_grad + back_sum
    hidden_grad = full_grad.astype(jnp.bfloat16)
    first_grad = (full_grad * silu_slope(first_pre)).astype(jnp.bfloat16)
    grad_w1_self = jnp.dot(features.T, first_grad, preferred_element_type=jnp.float32)
    grad_w1_near = jnp.dot(first_agg.T, first_grad, preferred_element_type=jnp.float32)
    grad_bias_one = jnp.sum(first_grad.astype(jnp.float32), axis=0)
    return (logits, hidden_grad, grad_w1_self, grad_w1_near, grad_bias_one, grad_w2_self, grad_w2_near, grad_bias_two)
```

```python
import functools

import jax
import jax.numpy as jnp
from jax import lax
from jax.experimental import pallas as pl
from jax.experimental.pallas import tpu as pltpu
from jax.sharding import PartitionSpec as P

AXES = ("dom", "sub", "feat")
CHIPS = ("dom", "sub")
SMEM = pl.BlockSpec(memory_space=pltpu.SMEM)
VMEM = pl.BlockSpec(memory_space=pltpu.VMEM)
ANY = pl.BlockSpec(memory_space=pl.ANY)
VMEM_LIMIT = 40 * 2**20
F32 = jnp.float32
BF16 = jnp.bfloat16


def struct(shape, dtype):
    return jax.ShapeDtypeStruct(shape, dtype)


def swapped(value, mask):
    pairs = [(source, source ^ mask) for source in range(lax.axis_size(AXES))]
    return lax.ppermute(value, AXES, pairs)


def dot(a, b):
    return jnp.dot(a, b, preferred_element_type=F32)


def dot_bt(a, b):
    return lax.dot_general(a, b, (((1,), (1,)), ((), ())), preferred_element_type=F32)


def run(body, in_specs, out_specs, out_shape, scratch, args, flops=0, moved=0):
    return pl.pallas_call(
        body,
        in_specs=in_specs,
        out_specs=out_specs,
        out_shape=out_shape,
        scratch_shapes=scratch,
        compiler_params=pltpu.CompilerParams(vmem_limit_bytes=VMEM_LIMIT),
        cost_estimate=pl.CostEstimate(flops=flops, bytes_accessed=moved, transcendentals=0),
    )(*args)


def pick_body(picked, *refs):
    indices = refs[: len(picked)]
    blocks = refs[len(picked)]
    outs = refs[len(picked) + 1 : -1]
    sems = refs[-1]
    copies = []
    for n, colour in enumerate(picked):
        for slot in range(outs[n].shape[0]):
            copies.append(
                pltpu.make_async_copy(
                    blocks.at[indices[n][0, colour, slot]], outs[n].at[slot], sems.at[len(copies)]
                )
            )
    for copy in copies:
        copy.start()
    for copy in copies:
        copy.wait()


def first_local_body(
    index, count, features, values, edges, w1_self, bias, near, own, features_t, values_t, edges_t
):
    tiles, fan = values.shape[0], values.shape[1]
    for t in range(tiles):
        left = jnp.concatenate([values[t, k] for k in range(fan)], axis=1)
        right = jnp.concatenate([features[index[t, k]] for k in range(fan)], axis=0)
        near[t] = dot(left, right)
        own[t] = dot(features[t], w1_self[...]) + bias[...]
        features_t[:, t * 128 : (t + 1) * 128] = features[t].T
        for k in range(fan):
            values_t[t, k] = values[t, k].T
    rounds, slots = edges.shape[0], edges.shape[1]
    for r in range(rounds):
        for s in range(slots):
            live = s < count[0, r]
            edges_t[r, s] = jnp.where(live, edges[r, s].T, jnp.zeros_like(edges[r, s]))


def add_boundary(total, whole_round, src, dst, count, edges, arrived):
    rounds, slots = edges.shape[0], edges.shape[1]
    spare = total.shape[0] - 1
    for r in range(rounds):
        for s in range(slots):
            where = jnp.where(s < count[0, r], dst[0, r, s], spare)
            tile = arrived[r][src[0, r, s]] if r == whole_round else arrived[r][s]
            total[where] = total[where] + dot(edges[r, s], tile)


def first_body(
    rounds, src, dst, count, *refs
):
    partner_src = refs[:rounds]
    arrived = refs[rounds : 2 * rounds]
    edges, near, own, w1_near, w2_near, first_agg, hidden, message = refs[2 * rounds : 2 * rounds + 8]
    sends = refs[2 * rounds + 8 : 3 * rounds + 8]
    total = refs[-1]
    tiles = near.shape[0]
    total[0:tiles] = near[...]
    add_boundary(total, rounds - 1, src, dst, count, edges, arrived)
    for t in range(tiles):
        agg = total[t].astype(BF16)
        first_agg[t] = agg
        pre = own[t] + dot(agg, w1_near[...])
        act = (pre * jax.nn.sigmoid(pre)).astype(BF16)
        hidden[t] = act
        message[t] = dot(act, w2_near[...]).astype(BF16)
    for r in range(rounds):
        for s in range(sends[r].shape[0]):
            sends[r][s] = message[partner_src[r][0, r, s]]


def second_local_body(
    index, labels, values, first_agg, own, hidden, message, w1_near, w2_self, bias,
    slope, near, target, first_agg_t, hidden_t,
):
    tiles, fan = values.shape[0], values.shape[1]
    classes = w2_self.shape[1]
    class_ids = lax.broadcasted_iota(jnp.int32, (classes, 128), 0)
    for t in range(tiles):
        left = jnp.concatenate([values[t, k] for k in range(fan)], axis=1)
        right = jnp.concatenate([message[index[t, k]] for k in range(fan)], axis=0)
        near[t] = dot(left, right) + dot(hidden[t], w2_self[...]) + bias[...]
        hot = (labels[t : t + 1, :] == class_ids).astype(F32)
        target[t] = hot.T
        pre = own[t] + dot(first_agg[t], w1_near[...])
        sig = jax.nn.sigmoid(pre)
        slope[t] = sig * (1.0 + pre * (1.0 - sig))
        first_agg_t[:, t * 128 : (t + 1) * 128] = first_agg[t].T
        hidden_t[:, t * 128 : (t + 1) * 128] = hidden[t].T


def second_body(rounds, src, dst, count, *refs):
    arrived = refs[:rounds]
    edges, edges_t, near, target, logits, error = refs[rounds : rounds + 6]
    sends = refs[rounds + 6 : 2 * rounds + 6]
    total = refs[-1]
    tiles = near.shape[0]
    total[0:tiles] = near[...]
    add_boundary(total, None, src, dst, count, edges, arrived)
    for t in range(tiles):
        pre = total[t]
        logits[t] = pre.astype(BF16)
        error[t] = (pre - target[t]).astype(BF16)
    for r in range(rounds):
        for s in range(sends[r].shape[0]):
            sends[r][s] = dot(edges_t[r, s], error[dst[0, r, s]]).astype(BF16)


def back_local_body(
    index, values_t, error, hidden_t, w2_self, back, self_grad, grad_w2_self, grad_bias_two
):
    tiles, fan = values_t.shape[0], values_t.shape[1]
    back[...] = jnp.zeros_like(back)
    bias = jnp.zeros((1, error.shape[2]), F32)
    for t in range(tiles):
        rows = error[t]
        for k in range(fan):
            where = index[t, k]
            back[where] = back[where] + dot(values_t[t, k], rows)
        self_grad[t] = dot_bt(rows, w2_self[...])
        bias = bias + jnp.sum(rows.astype(F32), axis=0, keepdims=True)
    grad_bias_two[...] = bias
    flat = error[...].reshape(tiles * error.shape[1], error.shape[2])
    grad_w2_self[...] = dot(hidden_t[...], flat)


def back_body(rounds, feat, *refs):
    partner_src = refs[:rounds]
    arrived = refs[rounds : 2 * rounds]
    (back, self_grad, slope, w2_near, features_t, first_agg_t, hidden_t, grad_w2_self, grad_bias_two,
     hidden_grad, send, keep, total, back_16, first_grad, packed) = refs[2 * rounds :]
    tiles, size, classes = back.shape
    width = self_grad.shape[2]
    total[...] = back[...]
    for r in range(rounds):
        for s in range(arrived[r].shape[0]):
            where = partner_src[r][0, r, s]
            total[where] = total[where] + arrived[r][s].astype(F32)
    bias = jnp.zeros((1, width), F32)
    for t in range(tiles):
        here = slice(t * size, (t + 1) * size)
        rows = total[t].astype(BF16)
        back_16[here, :] = rows
        full = self_grad[t] + dot_bt(rows, w2_near[...])
        hidden_grad[t] = full.astype(BF16)
        grad = (full * slope[t]).astype(BF16)
        first_grad[here, :] = grad
        bias = bias + jnp.sum(grad.astype(F32), axis=0, keepdims=True)
    deep = features_t.shape[0]
    at = 0
    for left in (features_t, first_agg_t):
        product = dot(left[...], first_grad[...])
        for c in range(width // 128):
            packed[at : at + deep, :] = product[:, c * 128 : (c + 1) * 128]
            at += deep
    packed[at : at + width, :] = grad_w2_self[...]
    at += width
    packed[at : at + width, :] = dot(hidden_t[...], back_16[...])
    at += width
    packed[at:, :] = jnp.zeros_like(packed[at:, :])
    for c in range(width // 128):
        packed[at + c : at + c + 1, :] = bias[:, c * 128 : (c + 1) * 128]
    at += width // 128
    packed[at : at + 1, :] = grad_bias_two[...]
    half = keep.shape[0]
    mine = feat[0]
    keep[...] = packed[pl.ds(pl.multiple_of(mine * half, 16), half), :]
    send[...] = packed[pl.ds(pl.multiple_of((1 - mine) * half, 16), half), :].astype(BF16)


def pair_body(keep, arrived, out):
    out[...] = (keep[...] + arrived[...].astype(F32)).astype(BF16)


def chips_body(arrived, out):
    chips = arrived.shape[0]
    total = arrived[0].astype(F32)
    for c in range(1, chips):
        total = total + arrived[c].astype(F32)
    total = total.astype(BF16)
    for c in range(chips):
        out[c] = total


def unpack_body(feat, mine, other, g1_self, g1_near, g1_bias, g2_self, g2_near, g2_bias, packed):
    half = mine.shape[0]
    packed[pl.ds(pl.multiple_of(feat[0] * half, 16), half), :] = mine[...].astype(F32)
    packed[pl.ds(pl.multiple_of((1 - feat[0]) * half, 16), half), :] = other[...].astype(F32)
    deep, width = g1_self.shape
    at = 0
    for out in (g1_self, g1_near):
        for c in range(width // 128):
            out[:, c * 128 : (c + 1) * 128] = packed[at : at + deep, :]
            at += deep
    for out in (g2_self, g2_near):
        out[...] = packed[at : at + width, :]
        at += width
    for c in range(width // 128):
        g1_bias[:, c * 128 : (c + 1) * 128] = packed[at : at + 1, :]
        at += 1
    g2_bias[...] = packed[at : at + 1, :]


def shards(
    features,
    labels,
    local_index,
    local_values,
    cross_src,
    cross_dst,
    cross_count,
    cross_values,
    w1_self,
    w1_near,
    bias_one,
    w2_self,
    w2_near,
    bias_two,
):
    tiles, fan, size, _ = local_values.shape
    rounds, slots = cross_src.shape[1], cross_src.shape[2]
    width_in = features.shape[1]
    hidden_width = w1_self.shape[1]
    classes = w2_self.shape[1]
    nodes = tiles * size
    total_bits = lax.axis_size(AXES).bit_length() - 1
    masks = [1 << (total_bits - 1 - colour) for colour in range(rounds)]
    chips = lax.axis_size(CHIPS)
    blocks = features.reshape(tiles, size, width_in)
    edges = cross_values[0]
    feat = lax.axis_index("feat").astype(jnp.int32).reshape(1)
    bias_one_row = bias_one.reshape(1, hidden_width)
    bias_two_row = bias_two.reshape(1, classes)
    label_rows = labels.reshape(tiles, size)

    whole = swapped(blocks, masks[-1])
    partner_src = [swapped(cross_src, mask) for mask in masks]
    picked = list(range(rounds - 1))
    picks = run(
        functools.partial(pick_body, picked),
        [SMEM] * len(picked) + [ANY],
        [ANY] * len(picked),
        [struct((slots, size, width_in), BF16)] * len(picked),
        [pltpu.SemaphoreType.DMA((len(picked) * slots,))],
        [partner_src[r] for r in picked] + [blocks],
        moved=2 * len(picked) * slots * size * width_in * 2,
    )
    arrived = [swapped(tile, masks[r]) for r, tile in zip(picked, picks)] + [whole]

    near, own, features_t, values_t, edges_t = run(
        first_local_body,
        [SMEM, SMEM] + [VMEM] * 5,
        [VMEM] * 5,
        [
            struct((tiles, size, width_in), F32),
            struct((tiles, size, hidden_width), F32),
            struct((width_in, nodes), BF16),
            struct(local_values.shape, BF16),
            struct(edges.shape, BF16),
        ],
        [],
        [local_index, cross_count, blocks, local_values, edges, w1_self, bias_one_row],
        flops=2 * nodes * width_in * (fan * size + hidden_width),
        moved=8 * 2**20,
    )

    first_agg, hidden, message, *sends = run(
        functools.partial(first_body, rounds),
        [SMEM] * (3 + rounds) + [VMEM] * (rounds + 5),
        [VMEM] * (3 + rounds),
        [
            struct((tiles, size, width_in), BF16),
            struct((tiles, size, hidden_width), BF16),
            struct((tiles, size, classes), BF16),
        ]
        + [struct((slots, size, classes), BF16)] * rounds,
        [pltpu.VMEM((tiles + 1, size, width_in), F32)],
        [cross_src, cross_dst, cross_count, *partner_src, *arrived, edges, near, own, w1_near, w2_near],
        flops=2 * nodes * width_in * (rounds * slots * size // tiles + hidden_width + classes),
        moved=8 * 2**20,
    )
    arrived = [swapped(tile, mask) for tile, mask in zip(sends, masks)]

    slope, near, target, first_agg_t, hidden_t = run(
        second_local_body,
        [SMEM] + [VMEM] * 9,
        [VMEM] * 5,
        [
            struct((tiles, size, hidden_width), F32),
            struct((tiles, size, classes), F32),
            struct((tiles, size, classes), F32),
            struct((width_in, nodes), BF16),
            struct((hidden_width, nodes), BF16),
        ],
        [],
        [local_index, label_rows, local_values, first_agg, own, hidden, message, w1_near, w2_self, bias_two_row],
        flops=2 * nodes * classes * (fan * size + 3 * hidden_width),
        moved=6 * 2**20,
    )

    logits, error, *sends = run(
        functools.partial(second_body, rounds),
        [SMEM] * 3 + [VMEM] * (rounds + 4),
        [VMEM] * (2 + rounds),
        [struct((tiles, size, classes), BF16), struct((tiles, size, classes), BF16)]
        + [struct((slots, size, classes), BF16)] * rounds,
        [pltpu.VMEM((tiles + 1, size, classes), F32)],
        [cross_src, cross_dst, cross_count, *arrived, edges, edges_t, near, target],
        flops=4 * rounds * slots * size * size * classes,
        moved=3 * 2**20,
    )
    arrived = [swapped(tile, mask) for tile, mask in zip(sends, masks)]

    back, self_grad, grad_w2_self, grad_bias_two = run(
        back_local_body,
        [SMEM] + [VMEM] * 4,
        [VMEM] * 4,
        [
            struct((tiles, size, classes), F32),
            struct((tiles, size, hidden_width), F32),
            struct((hidden_width, classes), F32),
            struct((1, classes), F32),
        ],
        [],
        [local_index, values_t, error, hidden_t, w2_self],
        flops=2 * nodes * classes * (fan * size + 2 * hidden_width),
        moved=4 * 2**20,
    )

    rows = (2 * width_in * hidden_width + 2 * hidden_width * classes + hidden_width + classes) // 128
    piece = -(-rows // (2 * chips * 16)) * 16
    half = piece * chips
    hidden_grad, send, keep = run(
        functools.partial(back_body, rounds),
        [SMEM] * (1 + rounds) + [VMEM] * (rounds + 9),
        [VMEM] * 3,
        [
            struct((tiles, size, hidden_width), BF16),
            struct((half, 128), BF16),
            struct((half, 128), F32),
        ],
        [
            pltpu.VMEM((tiles, size, classes), F32),
            pltpu.VMEM((nodes, classes), BF16),
            pltpu.VMEM((nodes, hidden_width), BF16),
            pltpu.VMEM((2 * half, 128), F32),
        ],
        [
            feat, *partner_src, *arrived, back, self_grad, slope, w2_near, features_t, first_agg_t,
            hidden_t, grad_w2_self, grad_bias_two,
        ],
        flops=2 * nodes * hidden_width * (2 * width_in + 2 * classes),
        moved=6 * 2**20,
    )

    pair = run(
        pair_body, [VMEM] * 2, VMEM, struct((half, 128), BF16), [],
        [keep, swapped(send, 1)], flops=half * 128, moved=half * 128 * 8,
    )
    pieces = lax.all_to_all(pair.reshape(chips, piece, 128), CHIPS, 0, 0)
    copies = run(
        chips_body, [VMEM], VMEM, struct((chips, piece, 128), BF16), [],
        [pieces], flops=half * 128, moved=half * 128 * 4,
    )
    mine = lax.all_to_all(copies, CHIPS, 0, 0).reshape(half, 128)
    other = swapped(mine, 1)
    g1_self, g1_near, g1_bias, g2_self, g2_near, g2_bias = run(
        unpack_body,
        [SMEM] + [VMEM] * 2,
        [VMEM] * 6,
        [
            struct((width_in, hidden_width), F32),
            struct((width_in, hidden_width), F32),
            struct((1, hidden_width), F32),
            struct((hidden_width, classes), F32),
            struct((hidden_width, classes), F32),
            struct((1, classes), F32),
        ],
        [pltpu.VMEM((2 * half, 128), F32)],
        [feat, mine, other],
        moved=half * 128 * 12,
    )
    return (
        logits.reshape(nodes, classes),
        hidden_grad.reshape(nodes, hidden_width),
        g1_self,
        g1_near,
        g1_bias.reshape(hidden_width),
        g2_self,
        g2_near,
        g2_bias.reshape(classes),
    )


def solution(mesh):
    in_specs = (
        P(("grp", "dom", "sub", "feat"), None),
        P(("grp", "dom", "sub", "feat")),
        P(("grp", "dom", "sub", "feat"), None),
        P(("grp", "dom", "sub", "feat"), None, None, None),
        P(("grp", "dom", "sub", "feat"), None, None),
        P(("grp", "dom", "sub", "feat"), None, None),
        P(("grp", "dom", "sub", "feat"), None),
        P(("grp", "dom", "sub", "feat"), None, None, None, None),
        P(),
        P(),
        P(),
        P(),
        P(),
        P(),
    )
    out_specs = (
        P(("grp", "dom", "sub", "feat"), None),
        P(("grp", "dom", "sub", "feat"), None),
        P("grp", None),
        P("grp", None),
        P("grp"),
        P("grp", None),
        P("grp", None),
        P("grp"),
    )
    return jax.shard_map(shards, mesh=mesh, in_specs=in_specs, out_specs=out_specs, check_vma=False)
```

```python
import functools

import jax
import jax.numpy as jnp
from jax import lax
from jax.experimental import pallas as pl
from jax.experimental.pallas import tpu as pltpu
from jax.sharding import PartitionSpec as P

AXES = ("dom", "sub", "feat")
CHIPS = ("dom", "sub")
SMEM = pl.BlockSpec(memory_space=pltpu.SMEM)
VMEM = pl.BlockSpec(memory_space=pltpu.VMEM)
VMEM_LIMIT = 8 * 2**20
F32 = jnp.float32
BF16 = jnp.bfloat16


def struct(shape, dtype):
    return jax.ShapeDtypeStruct(shape, dtype)


def swapped(value, mask):
    pairs = [(source, source ^ mask) for source in range(lax.axis_size(AXES))]
    return lax.ppermute(value, AXES, pairs)


def dot(a, b):
    return jnp.dot(a, b, preferred_element_type=F32)


def dot_bt(a, b):
    return lax.dot_general(a, b, (((1,), (1,)), ((), ())), preferred_element_type=F32)


def run(body, in_specs, out_specs, out_shape, scratch, args, flops=0, moved=0):
    return pl.pallas_call(
        body,
        in_specs=in_specs,
        out_specs=out_specs,
        out_shape=out_shape,
        scratch_shapes=scratch,
        compiler_params=pltpu.CompilerParams(vmem_limit_bytes=VMEM_LIMIT),
        cost_estimate=pl.CostEstimate(flops=flops, bytes_accessed=moved, transcendentals=0),
    )(*args)


class Table:
    def __init__(self, tiles, fan, rounds, slots):
        self.fan, self.slots = fan, slots
        self.where = tiles * fan
        self.dst = self.where + rounds * slots
        self.give = self.dst + rounds * slots
        self.feat = self.give + rounds * slots
        self.size = self.feat + 1

    def near_at(self, t, k):
        return t * self.fan + k

    def where_at(self, r, s):
        return self.where + r * self.slots + s

    def dst_at(self, r, s):
        return self.dst + r * self.slots + s

    def give_at(self, r, s):
        return self.give + r * self.slots + s


def stage_body(features, blocks, arrival):
    copy = pltpu.make_async_copy(features, blocks, arrival)
    copy.start()
    copy.wait()


def pick_body(rounds, *refs):
    partner_src = refs[:rounds]
    blocks = refs[rounds]
    outs = refs[rounds + 1 :]
    for r in range(rounds):
        for s in range(outs[r].shape[0]):
            outs[r][s] = blocks[partner_src[r][r, 0, s]]


def first_local_body(
    at, rounds, index, dst, count, feat, *refs
):
    partner_src = refs[:rounds]
    (features, values, edges, w1_self, bias, table, near, own, features_t, values_t,
     edges_t) = refs[rounds:]
    tiles, fan, size = values.shape[:3]
    slots = edges.shape[1]
    for t in range(tiles):
        for k in range(fan):
            table[at.near_at(t, k)] = index[k, t]
    for r in range(rounds):
        for s in range(slots):
            table[at.dst_at(r, s)] = dst[r, 0, s]
            table[at.where_at(r, s)] = jnp.where(s < count[0, r], dst[r, 0, s], tiles)
            table[at.give_at(r, s)] = partner_src[r][r, 0, s]
    table[at.feat] = feat[0]
    for t in range(tiles):
        left = jnp.concatenate([values[t, k] for k in range(fan)], axis=1)
        right = jnp.concatenate([features[index[k, t]] for k in range(fan)], axis=0)
        near[t] = dot(left, right)
        own[t] = dot(features[t], w1_self[...]) + bias[...]
        features_t[:, t * size : (t + 1) * size] = features[t].T
        for k in range(fan):
            values_t[t, k] = values[t, k].T
    for r in range(rounds):
        for s in range(slots):
            live = s < count[0, r]
            edges_t[r, s] = jnp.where(live, edges[r, s].T, jnp.zeros_like(edges[r, s]))


def add_boundary(at, total, table, edges, arrived):
    rounds, slots = edges.shape[0], edges.shape[1]
    for r in range(rounds):
        for s in range(slots):
            where = table[at.where_at(r, s)]
            total[where] = total[where] + dot(edges[r, s], arrived[r][s])


def first_body(at, rounds, table, *refs):
    arrived = refs[:rounds]
    edges, near, own, w1_near, w2_near, first_agg, hidden, message = refs[rounds : rounds + 8]
    sends = refs[rounds + 8 : 2 * rounds + 8]
    total = refs[-1]
    tiles = near.shape[0]
    total[0:tiles] = near[...]
    add_boundary(at, total, table, edges, arrived)
    for t in range(tiles):
        agg = total[t].astype(BF16)
        first_agg[t] = agg
        pre = own[t] + dot(agg, w1_near[...])
        act = (pre * jax.nn.sigmoid(pre)).astype(BF16)
        hidden[t] = act
        message[t] = dot(act, w2_near[...]).astype(BF16)
    for r in range(rounds):
        for s in range(sends[r].shape[0]):
            sends[r][s] = message[table[at.give_at(r, s)]]


def second_local_body(
    at, table, labels, values, first_agg, own, hidden, message, w1_near, w2_self, bias,
    slope, near, target, first_agg_t, hidden_t,
):
    tiles, fan = values.shape[0], values.shape[1]
    classes = w2_self.shape[1]
    class_ids = lax.broadcasted_iota(jnp.int32, (classes, 128), 0)
    for t in range(tiles):
        left = jnp.concatenate([values[t, k] for k in range(fan)], axis=1)
        right = jnp.concatenate([message[table[at.near_at(t, k)]] for k in range(fan)], axis=0)
        near[t] = dot(left, right) + dot(hidden[t], w2_self[...]) + bias[...]
        hot = (labels[t : t + 1, :] == class_ids).astype(F32)
        target[t] = hot.T
        pre = own[t] + dot(first_agg[t], w1_near[...])
        sig = jax.nn.sigmoid(pre)
        slope[t] = sig * (1.0 + pre * (1.0 - sig))
        first_agg_t[:, t * 128 : (t + 1) * 128] = first_agg[t].T
        hidden_t[:, t * 128 : (t + 1) * 128] = hidden[t].T


def second_body(at, rounds, table, *refs):
    arrived = refs[:rounds]
    edges, edges_t, near, target, logits, error = refs[rounds : rounds + 6]
    sends = refs[rounds + 6 : 2 * rounds + 6]
    total = refs[-1]
    tiles = near.shape[0]
    total[0:tiles] = near[...]
    add_boundary(at, total, table, edges, arrived)
    for t in range(tiles):
        pre = total[t]
        logits[t] = pre.astype(BF16)
        error[t] = (pre - target[t]).astype(BF16)
    for r in range(rounds):
        for s in range(sends[r].shape[0]):
            sends[r][s] = dot(edges_t[r, s], error[table[at.dst_at(r, s)]]).astype(BF16)


def back_local_body(
    at, table, values_t, error, hidden_t, w2_self, back, self_grad, grad_w2_self, grad_bias_two
):
    tiles, fan = values_t.shape[0], values_t.shape[1]
    back[...] = jnp.zeros_like(back)
    bias = jnp.zeros((1, error.shape[2]), F32)
    for t in range(tiles):
        rows = error[t]
        for k in range(fan):
            where = table[at.near_at(t, k)]
            back[where] = back[where] + dot(values_t[t, k], rows)
        self_grad[t] = dot_bt(rows, w2_self[...])
        bias = bias + jnp.sum(rows.astype(F32), axis=0, keepdims=True)
    grad_bias_two[...] = bias
    flat = error[...].reshape(tiles * error.shape[1], error.shape[2])
    grad_w2_self[...] = dot(hidden_t[...], flat)


def back_body(at, rounds, table, *refs):
    arrived = refs[:rounds]
    (back, self_grad, slope, w2_near, features_t, first_agg_t, hidden_t, grad_w2_self, grad_bias_two,
     hidden_grad, send, keep, total, back_16, first_grad, packed) = refs[rounds:]
    tiles, size, classes = back.shape
    width = self_grad.shape[2]
    total[...] = back[...]
    for r in range(rounds):
        for s in range(arrived[r].shape[0]):
            where = table[at.give_at(r, s)]
            total[where] = total[where] + arrived[r][s].astype(F32)
    bias = jnp.zeros((1, width), F32)
    for t in range(tiles):
        here = slice(t * size, (t + 1) * size)
        rows = total[t].astype(BF16)
        back_16[here, :] = rows
        full = self_grad[t] + dot_bt(rows, w2_near[...])
        hidden_grad[t] = full.astype(BF16)
        grad = (full * slope[t]).astype(BF16)
        first_grad[here, :] = grad
        bias = bias + jnp.sum(grad.astype(F32), axis=0, keepdims=True)
    deep = features_t.shape[0]
    row = 0
    for left in (features_t, first_agg_t):
        product = dot(left[...], first_grad[...])
        for c in range(width // 128):
            packed[row : row + deep, :] = product[:, c * 128 : (c + 1) * 128]
            row += deep
    packed[row : row + width, :] = grad_w2_self[...]
    row += width
    packed[row : row + width, :] = dot(hidden_t[...], back_16[...])
    row += width
    packed[row:, :] = jnp.zeros_like(packed[row:, :])
    for c in range(width // 128):
        packed[row + c : row + c + 1, :] = bias[:, c * 128 : (c + 1) * 128]
    row += width // 128
    packed[row : row + 1, :] = grad_bias_two[...]
    half = keep.shape[0]
    mine = table[at.feat]
    keep[...] = packed[pl.ds(pl.multiple_of(mine * half, 16), half), :]
    send[...] = packed[pl.ds(pl.multiple_of((1 - mine) * half, 16), half), :].astype(BF16)


def pair_body(keep, arrived, out):
    out[...] = (keep[...] + arrived[...].astype(F32)).astype(BF16)


def chips_body(arrived, out):
    chips = arrived.shape[0]
    total = arrived[0].astype(F32)
    for c in range(1, chips):
        total = total + arrived[c].astype(F32)
    total = total.astype(BF16)
    for c in range(chips):
        out[c] = total


def unpack_body(at, table, mine, other, g1_self, g1_near, g1_bias, g2_self, g2_near, g2_bias, packed):
    half = mine.shape[0]
    packed[pl.ds(pl.multiple_of(table[at.feat] * half, 16), half), :] = mine[...].astype(F32)
    packed[pl.ds(pl.multiple_of((1 - table[at.feat]) * half, 16), half), :] = other[...].astype(F32)
    deep, width = g1_self.shape
    row = 0
    for out in (g1_self, g1_near):
        for c in range(width // 128):
            out[:, c * 128 : (c + 1) * 128] = packed[row : row + deep, :]
            row += deep
    for out in (g2_self, g2_near):
        out[...] = packed[row : row + width, :]
        row += width
    for c in range(width // 128):
        g1_bias[:, c * 128 : (c + 1) * 128] = packed[row : row + 1, :]
        row += 1
    g2_bias[...] = packed[row : row + 1, :]


def shards(
    features,
    labels,
    local_index,
    local_values,
    cross_src,
    cross_dst,
    cross_count,
    cross_values,
    w1_self,
    w1_near,
    bias_one,
    w2_self,
    w2_near,
    bias_two,
):
    tiles, fan, size, _ = local_values.shape
    rounds, slots = cross_src.shape[1], cross_src.shape[2]
    width_in = features.shape[1]
    hidden_width = w1_self.shape[1]
    classes = w2_self.shape[1]
    nodes = tiles * size
    total_bits = lax.axis_size(AXES).bit_length() - 1
    masks = [1 << (total_bits - 1 - colour) for colour in range(rounds)]
    chips = lax.axis_size(CHIPS)
    blocks = features.reshape(tiles, size, width_in)
    edges = cross_values[0]
    feat = lax.axis_index("feat").astype(jnp.int32).reshape(1)
    bias_one_row = bias_one.reshape(1, hidden_width)
    bias_two_row = bias_two.reshape(1, classes)
    label_rows = labels.reshape(tiles, size)

    at = Table(tiles, fan, rounds, slots)

    reads = cross_src.transpose(1, 0, 2)
    partner_src = [swapped(reads, mask) for mask in masks]
    blocks = run(
        stage_body,
        [pl.BlockSpec(memory_space=pltpu.HBM)],
        VMEM,
        struct(blocks.shape, BF16),
        [pltpu.SemaphoreType.DMA],
        [blocks],
        moved=2 * nodes * width_in * 2,
    )
    picks = run(
        functools.partial(pick_body, rounds),
        [SMEM] * rounds + [VMEM],
        [VMEM] * rounds,
        [struct((slots, size, width_in), BF16)] * rounds,
        [],
        [*partner_src, blocks],
        moved=2 * rounds * slots * size * width_in * 2,
    )
    arrived = [swapped(tile, mask) for tile, mask in zip(picks, masks)]

    table, near, own, features_t, values_t, edges_t = run(
        functools.partial(first_local_body, at, rounds),
        [SMEM] * (4 + rounds) + [VMEM] * 5,
        [SMEM] + [VMEM] * 5,
        [
            struct((at.size,), jnp.int32),
            struct((tiles, size, width_in), F32),
            struct((tiles, size, hidden_width), F32),
            struct((width_in, nodes), BF16),
            struct(local_values.shape, BF16),
            struct(edges.shape, BF16),
        ],
        [],
        [
            local_index.T, cross_dst.transpose(1, 0, 2), cross_count, feat, *partner_src,
            blocks, local_values, edges, w1_self, bias_one_row,
        ],
        flops=2 * nodes * width_in * (fan * size + hidden_width),
        moved=8 * 2**20,
    )

    first_agg, hidden, message, *sends = run(
        functools.partial(first_body, at, rounds),
        [SMEM] + [VMEM] * (rounds + 5),
        [VMEM] * (3 + rounds),
        [
            struct((tiles, size, width_in), BF16),
            struct((tiles, size, hidden_width), BF16),
            struct((tiles, size, classes), BF16),
        ]
        + [struct((slots, size, classes), BF16)] * rounds,
        [pltpu.VMEM((tiles + 1, size, width_in), F32)],
        [table, *arrived, edges, near, own, w1_near, w2_near],
        flops=2 * nodes * width_in * (rounds * slots * size // tiles + hidden_width + classes),
        moved=8 * 2**20,
    )
    arrived = [swapped(tile, mask) for tile, mask in zip(sends, masks)]

    slope, near, target, first_agg_t, hidden_t = run(
        functools.partial(second_local_body, at),
        [SMEM] + [VMEM] * 9,
        [VMEM] * 5,
        [
            struct((tiles, size, hidden_width), F32),
            struct((tiles, size, classes), F32),
            struct((tiles, size, classes), F32),
            struct((width_in, nodes), BF16),
            struct((hidden_width, nodes), BF16),
        ],
        [],
        [table, label_rows, local_values, first_agg, own, hidden, message, w1_near, w2_self, bias_two_row],
        flops=2 * nodes * classes * (fan * size + 3 * hidden_width),
        moved=6 * 2**20,
    )

    logits, error, *sends = run(
        functools.partial(second_body, at, rounds),
        [SMEM] + [VMEM] * (rounds + 4),
        [VMEM] * (2 + rounds),
        [struct((tiles, size, classes), BF16), struct((tiles, size, classes), BF16)]
        + [struct((slots, size, classes), BF16)] * rounds,
        [pltpu.VMEM((tiles + 1, size, classes), F32)],
        [table, *arrived, edges, edges_t, near, target],
        flops=4 * rounds * slots * size * size * classes,
        moved=3 * 2**20,
    )
    arrived = [swapped(tile, mask) for tile, mask in zip(sends, masks)]

    back, self_grad, grad_w2_self, grad_bias_two = run(
        functools.partial(back_local_body, at),
        [SMEM] + [VMEM] * 4,
        [VMEM] * 4,
        [
            struct((tiles, size, classes), F32),
            struct((tiles, size, hidden_width), F32),
            struct((hidden_width, classes), F32),
            struct((1, classes), F32),
        ],
        [],
        [table, values_t, error, hidden_t, w2_self],
        flops=2 * nodes * classes * (fan * size + 2 * hidden_width),
        moved=4 * 2**20,
    )

    rows = (2 * width_in * hidden_width + 2 * hidden_width * classes + hidden_width + classes) // 128
    piece = -(-rows // (2 * chips * 16)) * 16
    half = piece * chips
    hidden_grad, send, keep = run(
        functools.partial(back_body, at, rounds),
        [SMEM] + [VMEM] * (rounds + 9),
        [VMEM] * 3,
        [
            struct((tiles, size, hidden_width), BF16),
            struct((half, 128), BF16),
            struct((half, 128), F32),
        ],
        [
            pltpu.VMEM((tiles, size, classes), F32),
            pltpu.VMEM((nodes, classes), BF16),
            pltpu.VMEM((nodes, hidden_width), BF16),
            pltpu.VMEM((2 * half, 128), F32),
        ],
        [
            table, *arrived, back, self_grad, slope, w2_near, features_t, first_agg_t,
            hidden_t, grad_w2_self, grad_bias_two,
        ],
        flops=2 * nodes * hidden_width * (2 * width_in + 2 * classes),
        moved=6 * 2**20,
    )

    pair = run(
        pair_body, [VMEM] * 2, VMEM, struct((half, 128), BF16), [],
        [keep, swapped(send, 1)], flops=half * 128, moved=half * 128 * 8,
    )
    pieces = lax.all_to_all(pair.reshape(chips, piece, 128), CHIPS, 0, 0)
    copies = run(
        chips_body, [VMEM], VMEM, struct((chips, piece, 128), BF16), [],
        [pieces], flops=half * 128, moved=half * 128 * 4,
    )
    mine = lax.all_to_all(copies, CHIPS, 0, 0).reshape(half, 128)
    other = swapped(mine, 1)
    g1_self, g1_near, g1_bias, g2_self, g2_near, g2_bias = run(
        functools.partial(unpack_body, at),
        [SMEM] + [VMEM] * 2,
        [VMEM] * 6,
        [
            struct((width_in, hidden_width), F32),
            struct((width_in, hidden_width), F32),
            struct((1, hidden_width), F32),
            struct((hidden_width, classes), F32),
            struct((hidden_width, classes), F32),
            struct((1, classes), F32),
        ],
        [pltpu.VMEM((2 * half, 128), F32)],
        [table, mine, other],
        moved=half * 128 * 12,
    )
    return (
        logits.reshape(nodes, classes),
        hidden_grad.reshape(nodes, hidden_width),
        g1_self,
        g1_near,
        g1_bias.reshape(hidden_width),
        g2_self,
        g2_near,
        g2_bias.reshape(classes),
    )


def solution(mesh):
    in_specs = (
        P(("grp", "dom", "sub", "feat"), None),
        P(("grp", "dom", "sub", "feat")),
        P(("grp", "dom", "sub", "feat"), None),
        P(("grp", "dom", "sub", "feat"), None, None, None),
        P(("grp", "dom", "sub", "feat"), None, None),
        P(("grp", "dom", "sub", "feat"), None, None),
        P(("grp", "dom", "sub", "feat"), None),
        P(("grp", "dom", "sub", "feat"), None, None, None, None),
        P(),
        P(),
        P(),
        P(),
        P(),
        P(),
    )
    out_specs = (
        P(("grp", "dom", "sub", "feat"), None),
        P(("grp", "dom", "sub", "feat"), None),
        P("grp", None),
        P("grp", None),
        P("grp"),
        P("grp", None),
        P("grp", None),
        P("grp"),
    )
    return jax.shard_map(shards, mesh=mesh, in_specs=in_specs, out_specs=out_specs, check_vma=False)
```

```python
import functools

import jax
import jax.numpy as jnp
from jax import lax
from jax.experimental import pallas as pl
from jax.experimental.pallas import tpu as pltpu
from jax.sharding import PartitionSpec as P

AXES = ("dom", "sub", "feat")
CHIPS = ("dom", "sub")
SMEM = pl.BlockSpec(memory_space=pltpu.SMEM)
VMEM = pl.BlockSpec(memory_space=pltpu.VMEM)
VMEM_LIMIT = 8 * 2**20
F32 = jnp.float32
BF16 = jnp.bfloat16


def struct(shape, dtype):
    return jax.ShapeDtypeStruct(shape, dtype)


def swapped(value, mask):
    pairs = [(source, source ^ mask) for source in range(lax.axis_size(AXES))]
    return lax.ppermute(value, AXES, pairs)


def dot(a, b):
    return jnp.dot(a, b, preferred_element_type=F32)


def dot_bt(a, b):
    return lax.dot_general(a, b, (((1,), (1,)), ((), ())), preferred_element_type=F32)


def run(body, in_specs, out_specs, out_shape, scratch, args, flops=0, moved=0):
    return pl.pallas_call(
        body,
        in_specs=in_specs,
        out_specs=out_specs,
        out_shape=out_shape,
        scratch_shapes=scratch,
        compiler_params=pltpu.CompilerParams(vmem_limit_bytes=VMEM_LIMIT),
        cost_estimate=pl.CostEstimate(flops=flops, bytes_accessed=moved, transcendentals=0),
    )(*args)


class Table:
    def __init__(self, tiles, fan, rounds, slots):
        self.fan, self.slots = fan, slots
        self.where = tiles * fan
        self.dst = self.where + rounds * slots
        self.give = self.dst + rounds * slots
        self.size = self.give + rounds * slots

    def near_at(self, t, k):
        return t * self.fan + k

    def where_at(self, r, s):
        return self.where + r * self.slots + s

    def dst_at(self, r, s):
        return self.dst + r * self.slots + s

    def give_at(self, r, s):
        return self.give + r * self.slots + s


def stage_body(features, blocks, arrival):
    copy = pltpu.make_async_copy(features, blocks, arrival)
    copy.start()
    copy.wait()


def pick_body(rounds, *refs):
    partner_src = refs[:rounds]
    blocks = refs[rounds]
    outs = refs[rounds + 1 :]
    for r in range(rounds):
        for s in range(outs[r].shape[0]):
            outs[r][s] = blocks[partner_src[r][r, 0, s]]


def first_local_body(
    at, rounds, index, dst, count, *refs
):
    partner_src = refs[:rounds]
    (features, values, edges, w1_self, bias, table, near, own, features_t, values_t,
     edges_t) = refs[rounds:]
    tiles, fan, size = values.shape[:3]
    slots = edges.shape[1]
    for t in range(tiles):
        for k in range(fan):
            table[at.near_at(t, k)] = index[k, t]
    for r in range(rounds):
        for s in range(slots):
            table[at.dst_at(r, s)] = dst[r, 0, s]
            table[at.where_at(r, s)] = jnp.where(s < count[0, r], dst[r, 0, s], tiles)
            table[at.give_at(r, s)] = partner_src[r][r, 0, s]
    for t in range(tiles):
        left = jnp.concatenate([values[t, k] for k in range(fan)], axis=1)
        right = jnp.concatenate([features[index[k, t]] for k in range(fan)], axis=0)
        near[t] = dot(left, right)
        own[t] = dot(features[t], w1_self[...]) + bias[...]
        features_t[:, t * size : (t + 1) * size] = features[t].T
        for k in range(fan):
            values_t[t, k] = values[t, k].T
    for r in range(rounds):
        for s in range(slots):
            live = s < count[0, r]
            edges_t[r, s] = jnp.where(live, edges[r, s].T, jnp.zeros_like(edges[r, s]))


def add_boundary(at, total, table, edges, arrived):
    rounds, slots = edges.shape[0], edges.shape[1]
    for r in range(rounds):
        for s in range(slots):
            where = table[at.where_at(r, s)]
            total[where] = total[where] + dot(edges[r, s], arrived[r][s])


def first_body(at, rounds, table, *refs):
    arrived = refs[:rounds]
    edges, near, own, w1_near, w2_near, first_agg, hidden, message = refs[rounds : rounds + 8]
    sends = refs[rounds + 8 : 2 * rounds + 8]
    total = refs[-1]
    tiles = near.shape[0]
    total[0:tiles] = near[...]
    add_boundary(at, total, table, edges, arrived)
    for t in range(tiles):
        agg = total[t].astype(BF16)
        first_agg[t] = agg
        pre = own[t] + dot(agg, w1_near[...])
        act = (pre * jax.nn.sigmoid(pre)).astype(BF16)
        hidden[t] = act
        message[t] = dot(act, w2_near[...]).astype(BF16)
    for r in range(rounds):
        for s in range(sends[r].shape[0]):
            sends[r][s] = message[table[at.give_at(r, s)]]


def second_local_body(
    at, table, labels, values, first_agg, own, hidden, message, w1_near, w2_self, bias,
    slope, near, target, first_agg_t, hidden_t,
):
    tiles, fan = values.shape[0], values.shape[1]
    classes = w2_self.shape[1]
    class_ids = lax.broadcasted_iota(jnp.int32, (classes, 128), 0)
    for t in range(tiles):
        left = jnp.concatenate([values[t, k] for k in range(fan)], axis=1)
        right = jnp.concatenate([message[table[at.near_at(t, k)]] for k in range(fan)], axis=0)
        near[t] = dot(left, right) + dot(hidden[t], w2_self[...]) + bias[...]
        hot = (labels[t : t + 1, :] == class_ids).astype(F32)
        target[t] = hot.T
        pre = own[t] + dot(first_agg[t], w1_near[...])
        sig = jax.nn.sigmoid(pre)
        slope[t] = sig * (1.0 + pre * (1.0 - sig))
        first_agg_t[:, t * 128 : (t + 1) * 128] = first_agg[t].T
        hidden_t[:, t * 128 : (t + 1) * 128] = hidden[t].T


def second_body(at, rounds, table, *refs):
    arrived = refs[:rounds]
    edges, edges_t, near, target, scores, error = refs[rounds : rounds + 6]
    sends = refs[rounds + 6 : 2 * rounds + 6]
    total = refs[-1]
    tiles = near.shape[0]
    total[0:tiles] = near[...]
    add_boundary(at, total, table, edges, arrived)
    for t in range(tiles):
        pre = total[t]
        scores[t] = pre.astype(BF16)
        error[t] = (pre - target[t]).astype(BF16)
    for r in range(rounds):
        for s in range(sends[r].shape[0]):
            sends[r][s] = dot(edges_t[r, s], error[table[at.dst_at(r, s)]]).astype(BF16)


def back_local_body(
    at, table, values_t, scores, error, hidden_t, w2_self,
    logits, back, self_grad, grad_w2_self, grad_bias_two,
):
    logits[...] = scores[...]
    tiles, fan = values_t.shape[0], values_t.shape[1]
    back[...] = jnp.zeros_like(back)
    bias = jnp.zeros((1, error.shape[2]), F32)
    for t in range(tiles):
        rows = error[t]
        for k in range(fan):
            where = table[at.near_at(t, k)]
            back[where] = back[where] + dot(values_t[t, k], rows)
        self_grad[t] = dot_bt(rows, w2_self[...])
        bias = bias + jnp.sum(rows.astype(F32), axis=0, keepdims=True)
    grad_bias_two[...] = bias
    flat = error[...].reshape(tiles * error.shape[1], error.shape[2])
    grad_w2_self[...] = dot(hidden_t[...], flat)


def back_body(at, rounds, table, *refs):
    arrived = refs[:rounds]
    (back, self_grad, slope, w2_near, features_t, first_agg_t, hidden_t, grad_w2_self, grad_bias_two,
     hidden_grad, send, keep, total, back_16, first_grad, packed) = refs[rounds:]
    tiles, size, classes = back.shape
    width = self_grad.shape[2]
    total[...] = back[...]
    for r in range(rounds):
        for s in range(arrived[r].shape[0]):
            where = table[at.give_at(r, s)]
            total[where] = total[where] + arrived[r][s].astype(F32)
    bias = jnp.zeros((1, width), F32)
    for t in range(tiles):
        here = slice(t * size, (t + 1) * size)
        rows = total[t].astype(BF16)
        back_16[here, :] = rows
        full = self_grad[t] + dot_bt(rows, w2_near[...])
        hidden_grad[t] = full.astype(BF16)
        grad = (full * slope[t]).astype(BF16)
        first_grad[here, :] = grad
        bias = bias + jnp.sum(grad.astype(F32), axis=0, keepdims=True)
    deep = features_t.shape[0]
    row = 0
    for left in (features_t, first_agg_t):
        product = dot(left[...], first_grad[...])
        for c in range(width // 128):
            packed[row : row + deep, :] = product[:, c * 128 : (c + 1) * 128]
            row += deep
    packed[row : row + width, :] = grad_w2_self[...]
    row += width
    packed[row : row + width, :] = dot(hidden_t[...], back_16[...])
    row += width
    packed[row:, :] = jnp.zeros_like(packed[row:, :])
    for c in range(width // 128):
        packed[row + c : row + c + 1, :] = bias[:, c * 128 : (c + 1) * 128]
    row += width // 128
    packed[row : row + 1, :] = grad_bias_two[...]
    half = keep.shape[0]
    mine = lax.axis_index("feat")
    keep[...] = packed[pl.ds(pl.multiple_of(mine * half, 16), half), :]
    send[...] = packed[pl.ds(pl.multiple_of((1 - mine) * half, 16), half), :].astype(BF16)


def leave_body(value, out):
    out[...] = value[...]


def pair_body(keep, arrived, out):
    out[...] = (keep[...] + arrived[...].astype(F32)).astype(BF16)


def chips_body(arrived, out):
    chips = arrived.shape[0]
    total = arrived[0].astype(F32)
    for c in range(1, chips):
        total = total + arrived[c].astype(F32)
    total = total.astype(BF16)
    for c in range(chips):
        out[c] = total


def unpack_body(mine, other, g1_self, g1_near, g1_bias, g2_self, g2_near, g2_bias, packed):
    half = mine.shape[0]
    feat = lax.axis_index("feat")
    packed[pl.ds(pl.multiple_of(feat * half, 16), half), :] = mine[...].astype(F32)
    packed[pl.ds(pl.multiple_of((1 - feat) * half, 16), half), :] = other[...].astype(F32)
    deep, width = g1_self.shape
    row = 0
    for out in (g1_self, g1_near):
        for c in range(width // 128):
            out[:, c * 128 : (c + 1) * 128] = packed[row : row + deep, :]
            row += deep
    for out in (g2_self, g2_near):
        out[...] = packed[row : row + width, :]
        row += width
    for c in range(width // 128):
        g1_bias[:, c * 128 : (c + 1) * 128] = packed[row : row + 1, :]
        row += 1
    g2_bias[...] = packed[row : row + 1, :]


def shards(
    features,
    labels,
    local_index,
    local_values,
    cross_src,
    cross_dst,
    cross_count,
    cross_values,
    w1_self,
    w1_near,
    bias_one,
    w2_self,
    w2_near,
    bias_two,
):
    tiles, fan, size, _ = local_values.shape
    rounds, slots = cross_src.shape[1], cross_src.shape[2]
    width_in = features.shape[1]
    hidden_width = w1_self.shape[1]
    classes = w2_self.shape[1]
    nodes = tiles * size
    total_bits = lax.axis_size(AXES).bit_length() - 1
    masks = [1 << (total_bits - 1 - colour) for colour in range(rounds)]
    chips = lax.axis_size(CHIPS)
    blocks = features.reshape(tiles, size, width_in)
    edges = cross_values[0]
    bias_one_row = bias_one.reshape(1, hidden_width)
    bias_two_row = bias_two.reshape(1, classes)
    label_rows = labels.reshape(tiles, size)

    at = Table(tiles, fan, rounds, slots)

    reads = cross_src.transpose(1, 0, 2)
    partner_src = [swapped(reads, mask) for mask in masks]
    blocks = run(
        stage_body,
        [pl.BlockSpec(memory_space=pltpu.HBM)],
        VMEM,
        struct(blocks.shape, BF16),
        [pltpu.SemaphoreType.DMA],
        [blocks],
        moved=2 * nodes * width_in * 2,
    )
    picks = run(
        functools.partial(pick_body, rounds),
        [SMEM] * rounds + [VMEM],
        [VMEM] * rounds,
        [struct((slots, size, width_in), BF16)] * rounds,
        [],
        [*partner_src, blocks],
        moved=2 * rounds * slots * size * width_in * 2,
    )
    arrived = [swapped(tile, mask) for tile, mask in zip(picks, masks)]

    table, near, own, features_t, values_t, edges_t = run(
        functools.partial(first_local_body, at, rounds),
        [SMEM] * (3 + rounds) + [VMEM] * 5,
        [SMEM] + [VMEM] * 5,
        [
            struct((at.size,), jnp.int32),
            struct((tiles, size, width_in), F32),
            struct((tiles, size, hidden_width), F32),
            struct((width_in, nodes), BF16),
            struct(local_values.shape, BF16),
            struct(edges.shape, BF16),
        ],
        [],
        [
            local_index.T, cross_dst.transpose(1, 0, 2), cross_count, *partner_src,
            blocks, local_values, edges, w1_self, bias_one_row,
        ],
        flops=2 * nodes * width_in * (fan * size + hidden_width),
        moved=8 * 2**20,
    )

    first_agg, hidden, message, *sends = run(
        functools.partial(first_body, at, rounds),
        [SMEM] + [VMEM] * (rounds + 5),
        [VMEM] * (3 + rounds),
        [
            struct((tiles, size, width_in), BF16),
            struct((tiles, size, hidden_width), BF16),
            struct((tiles, size, classes), BF16),
        ]
        + [struct((slots, size, classes), BF16)] * rounds,
        [pltpu.VMEM((tiles + 1, size, width_in), F32)],
        [table, *arrived, edges, near, own, w1_near, w2_near],
        flops=2 * nodes * width_in * (rounds * slots * size // tiles + hidden_width + classes),
        moved=8 * 2**20,
    )
    arrived = [swapped(tile, mask) for tile, mask in zip(sends, masks)]

    slope, near, target, first_agg_t, hidden_t = run(
        functools.partial(second_local_body, at),
        [SMEM] + [VMEM] * 9,
        [VMEM] * 5,
        [
            struct((tiles, size, hidden_width), F32),
            struct((tiles, size, classes), F32),
            struct((tiles, size, classes), F32),
            struct((width_in, nodes), BF16),
            struct((hidden_width, nodes), BF16),
        ],
        [],
        [table, label_rows, local_values, first_agg, own, hidden, message, w1_near, w2_self, bias_two_row],
        flops=2 * nodes * classes * (fan * size + 3 * hidden_width),
        moved=6 * 2**20,
    )

    scores, error, *sends = run(
        functools.partial(second_body, at, rounds),
        [SMEM] + [VMEM] * (rounds + 4),
        [VMEM] * (2 + rounds),
        [struct((tiles, size, classes), BF16), struct((tiles, size, classes), BF16)]
        + [struct((slots, size, classes), BF16)] * rounds,
        [pltpu.VMEM((tiles + 1, size, classes), F32)],
        [table, *arrived, edges, edges_t, near, target],
        flops=4 * rounds * slots * size * size * classes,
        moved=3 * 2**20,
    )
    arrived = [swapped(tile, mask) for tile, mask in zip(sends, masks)]

    logits, back, self_grad, grad_w2_self, grad_bias_two = run(
        functools.partial(back_local_body, at),
        [SMEM] + [VMEM] * 5,
        [VMEM] * 5,
        [
            struct((tiles, size, classes), BF16),
            struct((tiles, size, classes), F32),
            struct((tiles, size, hidden_width), F32),
            struct((hidden_width, classes), F32),
            struct((1, classes), F32),
        ],
        [],
        [table, values_t, scores, error, hidden_t, w2_self],
        flops=2 * nodes * classes * (fan * size + 2 * hidden_width),
        moved=4 * 2**20,
    )

    rows = (2 * width_in * hidden_width + 2 * hidden_width * classes + hidden_width + classes) // 128
    piece = -(-rows // (2 * chips * 16)) * 16
    half = piece * chips
    hidden_grad, send, keep = run(
        functools.partial(back_body, at, rounds),
        [SMEM] + [VMEM] * (rounds + 9),
        [VMEM] * 3,
        [
            struct((tiles, size, hidden_width), BF16),
            struct((half, 128), BF16),
            struct((half, 128), F32),
        ],
        [
            pltpu.VMEM((tiles, size, classes), F32),
            pltpu.VMEM((nodes, classes), BF16),
            pltpu.VMEM((nodes, hidden_width), BF16),
            pltpu.VMEM((2 * half, 128), F32),
        ],
        [
            table, *arrived, back, self_grad, slope, w2_near, features_t, first_agg_t,
            hidden_t, grad_w2_self, grad_bias_two,
        ],
        flops=2 * nodes * hidden_width * (2 * width_in + 2 * classes),
        moved=6 * 2**20,
    )

    arrived = swapped(send, 1)
    hidden_grad = run(
        leave_body, [VMEM], VMEM, struct(hidden_grad.shape, BF16), [],
        [hidden_grad], moved=4 * nodes * hidden_width,
    )

    pair = run(
        pair_body, [VMEM] * 2, VMEM, struct((half, 128), BF16), [],
        [keep, arrived], flops=half * 128, moved=half * 128 * 8,
    )
    pieces = lax.all_to_all(pair.reshape(chips, piece, 128), CHIPS, 0, 0)
    copies = run(
        chips_body, [VMEM], VMEM, struct((chips, piece, 128), BF16), [],
        [pieces], flops=half * 128, moved=half * 128 * 4,
    )
    mine = lax.all_to_all(copies, CHIPS, 0, 0).reshape(half, 128)
    other = swapped(mine, 1)
    g1_self, g1_near, g1_bias, g2_self, g2_near, g2_bias = run(
        unpack_body,
        [VMEM] * 2,
        [VMEM] * 6,
        [
            struct((width_in, hidden_width), F32),
            struct((width_in, hidden_width), F32),
            struct((1, hidden_width), F32),
            struct((hidden_width, classes), F32),
            struct((hidden_width, classes), F32),
            struct((1, classes), F32),
        ],
        [pltpu.VMEM((2 * half, 128), F32)],
        [mine, other],
        moved=half * 128 * 12,
    )
    return (
        logits.reshape(nodes, classes),
        hidden_grad.reshape(nodes, hidden_width),
        g1_self,
        g1_near,
        g1_bias.reshape(hidden_width),
        g2_self,
        g2_near,
        g2_bias.reshape(classes),
    )


def solution(mesh):
    in_specs = (
        P(("grp", "dom", "sub", "feat"), None),
        P(("grp", "dom", "sub", "feat")),
        P(("grp", "dom", "sub", "feat"), None),
        P(("grp", "dom", "sub", "feat"), None, None, None),
        P(("grp", "dom", "sub", "feat"), None, None),
        P(("grp", "dom", "sub", "feat"), None, None),
        P(("grp", "dom", "sub", "feat"), None),
        P(("grp", "dom", "sub", "feat"), None, None, None, None),
        P(),
        P(),
        P(),
        P(),
        P(),
        P(),
    )
    out_specs = (
        P(("grp", "dom", "sub", "feat"), None),
        P(("grp", "dom", "sub", "feat"), None),
        P("grp", None),
        P("grp", None),
        P("grp"),
        P("grp", None),
        P("grp", None),
        P("grp"),
    )
    return jax.shard_map(shards, mesh=mesh, in_specs=in_specs, out_specs=out_specs, check_vma=False)
```

```python
import functools

import jax
import jax.numpy as jnp
from jax import lax
from jax.experimental import pallas as pl
from jax.experimental.pallas import tpu as pltpu
from jax.sharding import PartitionSpec as P

AXES = ("dom", "sub", "feat")
CHIPS = ("dom", "sub")
SMEM = pl.BlockSpec(memory_space=pltpu.SMEM)
VMEM = pl.BlockSpec(memory_space=pltpu.VMEM)
VMEM_LIMIT = 8 * 2**20
F32 = jnp.float32
BF16 = jnp.bfloat16


def struct(shape, dtype):
    return jax.ShapeDtypeStruct(shape, dtype)


def swapped(value, mask):
    pairs = [(source, source ^ mask) for source in range(lax.axis_size(AXES))]
    return lax.ppermute(value, AXES, pairs)


def dot(a, b):
    return jnp.dot(a, b, preferred_element_type=F32)


def dot_bt(a, b):
    return lax.dot_general(a, b, (((1,), (1,)), ((), ())), preferred_element_type=F32)


def run(body, in_specs, out_specs, out_shape, scratch, args, flops=0, moved=0):
    return pl.pallas_call(
        body,
        in_specs=in_specs,
        out_specs=out_specs,
        out_shape=out_shape,
        scratch_shapes=scratch,
        compiler_params=pltpu.CompilerParams(vmem_limit_bytes=VMEM_LIMIT),
        cost_estimate=pl.CostEstimate(flops=flops, bytes_accessed=moved, transcendentals=0),
    )(*args)


class Table:
    def __init__(self, tiles, fan, rounds, slots):
        self.fan, self.slots = fan, slots
        self.where = tiles * fan
        self.dst = self.where + rounds * slots
        self.give = self.dst + rounds * slots
        self.size = self.give + rounds * slots

    def near_at(self, t, k):
        return t * self.fan + k

    def where_at(self, r, s):
        return self.where + r * self.slots + s

    def dst_at(self, r, s):
        return self.dst + r * self.slots + s

    def give_at(self, r, s):
        return self.give + r * self.slots + s


def stage_body(features, blocks, arrival):
    copy = pltpu.make_async_copy(features, blocks, arrival)
    copy.start()
    copy.wait()


def pick_body(rounds, *refs):
    partner_src = refs[:rounds]
    blocks = refs[rounds]
    outs = refs[rounds + 1 :]
    for r in range(rounds):
        row = partner_src[r][r]
        for s in range(outs[r].shape[0]):
            outs[r][s] = blocks[row[0, s]]


def first_local_body(
    at, rounds, index, dst, count, *refs
):
    partner_src = refs[:rounds]
    (features, values, edges, w1_self, bias, table, near, own, features_t, values_t,
     edges_t) = refs[rounds:]
    tiles, fan, size = values.shape[:3]
    slots = edges.shape[1]
    for t in range(tiles):
        for k in range(fan):
            table[at.near_at(t, k)] = index[k, t]
    for r in range(rounds):
        for s in range(slots):
            table[at.dst_at(r, s)] = dst[r, 0, s]
            table[at.where_at(r, s)] = jnp.where(s < count[0, r], dst[r, 0, s], tiles)
            table[at.give_at(r, s)] = partner_src[r][r, 0, s]
    for t in range(tiles):
        left = jnp.concatenate([values[t, k] for k in range(fan)], axis=1)
        right = jnp.concatenate([features[index[k, t]] for k in range(fan)], axis=0)
        near[t] = dot(left, right)
        own[t] = dot(features[t], w1_self[...]) + bias[...]
        features_t[:, t * size : (t + 1) * size] = features[t].T
        for k in range(fan):
            values_t[t, k] = values[t, k].T
    for r in range(rounds):
        for s in range(slots):
            live = s < count[0, r]
            edges_t[r, s] = jnp.where(live, edges[r, s].T, jnp.zeros_like(edges[r, s]))


def add_boundary(at, total, table, edges, arrived):
    rounds, slots = edges.shape[0], edges.shape[1]
    for r in range(rounds):
        for s in range(slots):
            where = table[at.where_at(r, s)]
            total[where] = total[where] + dot(edges[r, s], arrived[r][s])


def first_body(at, rounds, table, *refs):
    arrived = refs[:rounds]
    edges, near, own, w1_near, w2_near, first_agg, hidden, message = refs[rounds : rounds + 8]
    sends = refs[rounds + 8 : 2 * rounds + 8]
    total = refs[-1]
    tiles = near.shape[0]
    total[0:tiles] = near[...]
    add_boundary(at, total, table, edges, arrived)
    for t in range(tiles):
        agg = total[t].astype(BF16)
        first_agg[t] = agg
        pre = own[t] + dot(agg, w1_near[...])
        act = (pre * jax.nn.sigmoid(pre)).astype(BF16)
        hidden[t] = act
        message[t] = dot(act, w2_near[...]).astype(BF16)
    for r in range(rounds):
        for s in range(sends[r].shape[0]):
            sends[r][s] = message[table[at.give_at(r, s)]]


def second_local_body(
    at, table, labels, values, first_agg, own, hidden, message, w1_near, w2_self, bias,
    slope, near, target, first_agg_t, hidden_t,
):
    tiles, fan = values.shape[0], values.shape[1]
    classes = w2_self.shape[1]
    class_ids = lax.broadcasted_iota(jnp.int32, (classes, 128), 0)
    for t in range(tiles):
        left = jnp.concatenate([values[t, k] for k in range(fan)], axis=1)
        right = jnp.concatenate([message[table[at.near_at(t, k)]] for k in range(fan)], axis=0)
        near[t] = dot(left, right) + dot(hidden[t], w2_self[...]) + bias[...]
        hot = (labels[t : t + 1, :] == class_ids).astype(F32)
        target[t] = hot.T
        pre = own[t] + dot(first_agg[t], w1_near[...])
        sig = jax.nn.sigmoid(pre)
        slope[t] = sig * (1.0 + pre * (1.0 - sig))
        first_agg_t[:, t * 128 : (t + 1) * 128] = first_agg[t].T
        hidden_t[:, t * 128 : (t + 1) * 128] = hidden[t].T


def second_body(at, rounds, table, *refs):
    arrived = refs[:rounds]
    edges, edges_t, near, target, scores, error = refs[rounds : rounds + 6]
    sends = refs[rounds + 6 : 2 * rounds + 6]
    total = refs[-1]
    tiles = near.shape[0]
    total[0:tiles] = near[...]
    add_boundary(at, total, table, edges, arrived)
    for t in range(tiles):
        pre = total[t]
        scores[t] = pre.astype(BF16)
        error[t] = (pre - target[t]).astype(BF16)
    for r in range(rounds):
        for s in range(sends[r].shape[0]):
            sends[r][s] = dot(edges_t[r, s], error[table[at.dst_at(r, s)]]).astype(BF16)


def back_local_body(
    at, table, values_t, scores, error, hidden_t, w2_self,
    logits, back, self_grad, grad_w2_self, grad_bias_two,
):
    logits[...] = scores[...]
    tiles, fan = values_t.shape[0], values_t.shape[1]
    back[...] = jnp.zeros_like(back)
    bias = jnp.zeros((1, error.shape[2]), F32)
    for t in range(tiles):
        rows = error[t]
        for k in range(fan):
            where = table[at.near_at(t, k)]
            back[where] = back[where] + dot(values_t[t, k], rows)
        self_grad[t] = dot_bt(rows, w2_self[...])
        bias = bias + jnp.sum(rows.astype(F32), axis=0, keepdims=True)
    grad_bias_two[...] = bias
    flat = error[...].reshape(tiles * error.shape[1], error.shape[2])
    grad_w2_self[...] = dot(hidden_t[...], flat)


def back_body(at, rounds, table, *refs):
    arrived = refs[:rounds]
    (back, self_grad, slope, w2_near, features_t, first_agg_t, hidden_t, grad_w2_self, grad_bias_two,
     hidden_grad, send, keep, total, back_16, first_grad, packed) = refs[rounds:]
    tiles, size, classes = back.shape
    width = self_grad.shape[2]
    total[...] = back[...]
    for r in range(rounds):
        for s in range(arrived[r].shape[0]):
            where = table[at.give_at(r, s)]
            total[where] = total[where] + arrived[r][s].astype(F32)
    bias = jnp.zeros((1, width), F32)
    for t in range(tiles):
        here = slice(t * size, (t + 1) * size)
        rows = total[t].astype(BF16)
        back_16[here, :] = rows
        full = self_grad[t] + dot_bt(rows, w2_near[...])
        hidden_grad[t] = full.astype(BF16)
        grad = (full * slope[t]).astype(BF16)
        first_grad[here, :] = grad
        bias = bias + jnp.sum(grad.astype(F32), axis=0, keepdims=True)
    deep = features_t.shape[0]
    row = 0
    for left in (features_t, first_agg_t):
        product = dot(left[...], first_grad[...])
        for c in range(width // 128):
            packed[row : row + deep, :] = product[:, c * 128 : (c + 1) * 128]
            row += deep
    packed[row : row + width, :] = grad_w2_self[...]
    row += width
    packed[row : row + width, :] = dot(hidden_t[...], back_16[...])
    row += width
    packed[row:, :] = jnp.zeros_like(packed[row:, :])
    for c in range(width // 128):
        packed[row + c : row + c + 1, :] = bias[:, c * 128 : (c + 1) * 128]
    row += width // 128
    packed[row : row + 1, :] = grad_bias_two[...]
    half = keep.shape[0]
    mine = lax.axis_index("feat")
    keep[...] = packed[pl.ds(pl.multiple_of(mine * half, 16), half), :]
    send[...] = packed[pl.ds(pl.multiple_of((1 - mine) * half, 16), half), :].astype(BF16)


def leave_body(value, out):
    out[...] = value[...]


def pair_body(keep, arrived, out):
    out[...] = (keep[...] + arrived[...].astype(F32)).astype(BF16)


def chips_body(arrived, out):
    chips = arrived.shape[0]
    total = arrived[0].astype(F32)
    for c in range(1, chips):
        total = total + arrived[c].astype(F32)
    total = total.astype(BF16)
    for c in range(chips):
        out[c] = total


def unpack_body(mine, other, g1_self, g1_near, g1_bias, g2_self, g2_near, g2_bias, packed):
    half = mine.shape[0]
    feat = lax.axis_index("feat")
    packed[pl.ds(pl.multiple_of(feat * half, 16), half), :] = mine[...].astype(F32)
    packed[pl.ds(pl.multiple_of((1 - feat) * half, 16), half), :] = other[...].astype(F32)
    deep, width = g1_self.shape
    row = 0
    for out in (g1_self, g1_near):
        for c in range(width // 128):
            out[:, c * 128 : (c + 1) * 128] = packed[row : row + deep, :]
            row += deep
    for out in (g2_self, g2_near):
        out[...] = packed[row : row + width, :]
        row += width
    for c in range(width // 128):
        g1_bias[:, c * 128 : (c + 1) * 128] = packed[row : row + 1, :]
        row += 1
    g2_bias[...] = packed[row : row + 1, :]


def shards(
    features,
    labels,
    local_index,
    local_values,
    cross_src,
    cross_dst,
    cross_count,
    cross_values,
    w1_self,
    w1_near,
    bias_one,
    w2_self,
    w2_near,
    bias_two,
):
    tiles, fan, size, _ = local_values.shape
    rounds, slots = cross_src.shape[1], cross_src.shape[2]
    width_in = features.shape[1]
    hidden_width = w1_self.shape[1]
    classes = w2_self.shape[1]
    nodes = tiles * size
    total_bits = lax.axis_size(AXES).bit_length() - 1
    masks = [1 << (total_bits - 1 - colour) for colour in range(rounds)]
    chips = lax.axis_size(CHIPS)
    blocks = features.reshape(tiles, size, width_in)
    edges = cross_values[0]
    bias_one_row = bias_one.reshape(1, hidden_width)
    bias_two_row = bias_two.reshape(1, classes)
    label_rows = labels.reshape(tiles, size)

    at = Table(tiles, fan, rounds, slots)

    reads = cross_src.transpose(1, 0, 2)
    partner_src = [swapped(reads, mask) for mask in masks]
    blocks = run(
        stage_body,
        [pl.BlockSpec(memory_space=pltpu.HBM)],
        VMEM,
        struct(blocks.shape, BF16),
        [pltpu.SemaphoreType.DMA],
        [blocks],
        moved=2 * nodes * width_in * 2,
    )
    picks = run(
        functools.partial(pick_body, rounds),
        [VMEM] * rounds + [VMEM],
        [VMEM] * rounds,
        [struct((slots, size, width_in), BF16)] * rounds,
        [],
        [*partner_src, blocks],
        moved=2 * rounds * slots * size * width_in * 2,
    )
    arrived = [swapped(tile, mask) for tile, mask in zip(picks, masks)]

    table, near, own, features_t, values_t, edges_t = run(
        functools.partial(first_local_body, at, rounds),
        [SMEM] * (3 + rounds) + [VMEM] * 5,
        [SMEM] + [VMEM] * 5,
        [
            pltpu.SMEM((at.size,), jnp.int32),
            struct((tiles, size, width_in), F32),
            struct((tiles, size, hidden_width), F32),
            struct((width_in, nodes), BF16),
            struct(local_values.shape, BF16),
            struct(edges.shape, BF16),
        ],
        [],
        [
            local_index.T, cross_dst.transpose(1, 0, 2), cross_count, *partner_src,
            blocks, local_values, edges, w1_self, bias_one_row,
        ],
        flops=2 * nodes * width_in * (fan * size + hidden_width),
        moved=8 * 2**20,
    )

    first_agg, hidden, message, *sends = run(
        functools.partial(first_body, at, rounds),
        [SMEM] + [VMEM] * (rounds + 5),
        [VMEM] * (3 + rounds),
        [
            struct((tiles, size, width_in), BF16),
            struct((tiles, size, hidden_width), BF16),
            struct((tiles, size, classes), BF16),
        ]
        + [struct((slots, size, classes), BF16)] * rounds,
        [pltpu.VMEM((tiles + 1, size, width_in), F32)],
        [table, *arrived, edges, near, own, w1_near, w2_near],
        flops=2 * nodes * width_in * (rounds * slots * size // tiles + hidden_width + classes),
        moved=8 * 2**20,
    )
    arrived = [swapped(tile, mask) for tile, mask in zip(sends, masks)]

    slope, near, target, first_agg_t, hidden_t = run(
        functools.partial(second_local_body, at),
        [SMEM] + [VMEM] * 9,
        [VMEM] * 5,
        [
            struct((tiles, size, hidden_width), F32),
            struct((tiles, size, classes), F32),
            struct((tiles, size, classes), F32),
            struct((width_in, nodes), BF16),
            struct((hidden_width, nodes), BF16),
        ],
        [],
        [table, label_rows, local_values, first_agg, own, hidden, message, w1_near, w2_self, bias_two_row],
        flops=2 * nodes * classes * (fan * size + 3 * hidden_width),
        moved=6 * 2**20,
    )

    scores, error, *sends = run(
        functools.partial(second_body, at, rounds),
        [SMEM] + [VMEM] * (rounds + 4),
        [VMEM] * (2 + rounds),
        [struct((tiles, size, classes), BF16), struct((tiles, size, classes), BF16)]
        + [struct((slots, size, classes), BF16)] * rounds,
        [pltpu.VMEM((tiles + 1, size, classes), F32)],
        [table, *arrived, edges, edges_t, near, target],
        flops=4 * rounds * slots * size * size * classes,
        moved=3 * 2**20,
    )
    arrived = [swapped(tile, mask) for tile, mask in zip(sends, masks)]

    logits, back, self_grad, grad_w2_self, grad_bias_two = run(
        functools.partial(back_local_body, at),
        [SMEM] + [VMEM] * 5,
        [VMEM] * 5,
        [
            struct((tiles, size, classes), BF16),
            struct((tiles, size, classes), F32),
            struct((tiles, size, hidden_width), F32),
            struct((hidden_width, classes), F32),
            struct((1, classes), F32),
        ],
        [],
        [table, values_t, scores, error, hidden_t, w2_self],
        flops=2 * nodes * classes * (fan * size + 2 * hidden_width),
        moved=4 * 2**20,
    )

    rows = (2 * width_in * hidden_width + 2 * hidden_width * classes + hidden_width + classes) // 128
    piece = -(-rows // (2 * chips * 8)) * 8
    half = piece * chips
    hidden_grad, send, keep = run(
        functools.partial(back_body, at, rounds),
        [SMEM] + [VMEM] * (rounds + 9),
        [VMEM] * 3,
        [
            struct((tiles, size, hidden_width), BF16),
            struct((half, 128), BF16),
            struct((half, 128), F32),
        ],
        [
            pltpu.VMEM((tiles, size, classes), F32),
            pltpu.VMEM((nodes, classes), BF16),
            pltpu.VMEM((nodes, hidden_width), BF16),
            pltpu.VMEM((2 * half, 128), F32),
        ],
        [
            table, *arrived, back, self_grad, slope, w2_near, features_t, first_agg_t,
            hidden_t, grad_w2_self, grad_bias_two,
        ],
        flops=2 * nodes * hidden_width * (2 * width_in + 2 * classes),
        moved=6 * 2**20,
    )

    arrived = swapped(send, 1)
    hidden_grad = run(
        leave_body, [VMEM], VMEM, struct(hidden_grad.shape, BF16), [],
        [hidden_grad], moved=4 * nodes * hidden_width,
    )

    pair = run(
        pair_body, [VMEM] * 2, VMEM, struct((half, 128), BF16), [],
        [keep, arrived], flops=half * 128, moved=half * 128 * 8,
    )
    pieces = lax.all_to_all(pair.reshape(chips, piece, 128), CHIPS, 0, 0)
    copies = run(
        chips_body, [VMEM], VMEM, struct((chips, piece, 128), BF16), [],
        [pieces], flops=half * 128, moved=half * 128 * 4,
    )
    mine = lax.all_to_all(copies, CHIPS, 0, 0).reshape(half, 128)
    other = swapped(mine, 1)
    g1_self, g1_near, g1_bias, g2_self, g2_near, g2_bias = run(
        unpack_body,
        [VMEM] * 2,
        [VMEM] * 6,
        [
            struct((width_in, hidden_width), F32),
            struct((width_in, hidden_width), F32),
            struct((1, hidden_width), F32),
            struct((hidden_width, classes), F32),
            struct((hidden_width, classes), F32),
            struct((1, classes), F32),
        ],
        [pltpu.VMEM((2 * half, 128), F32)],
        [mine, other],
        moved=half * 128 * 12,
    )
    return (
        logits.reshape(nodes, classes),
        hidden_grad.reshape(nodes, hidden_width),
        g1_self,
        g1_near,
        g1_bias.reshape(hidden_width),
        g2_self,
        g2_near,
        g2_bias.reshape(classes),
    )


def solution(mesh):
    in_specs = (
        P(("grp", "dom", "sub", "feat"), None),
        P(("grp", "dom", "sub", "feat")),
        P(("grp", "dom", "sub", "feat"), None),
        P(("grp", "dom", "sub", "feat"), None, None, None),
        P(("grp", "dom", "sub", "feat"), None, None),
        P(("grp", "dom", "sub", "feat"), None, None),
        P(("grp", "dom", "sub", "feat"), None),
        P(("grp", "dom", "sub", "feat"), None, None, None, None),
        P(),
        P(),
        P(),
        P(),
        P(),
        P(),
    )
    out_specs = (
        P(("grp", "dom", "sub", "feat"), None),
        P(("grp", "dom", "sub", "feat"), None),
        P("grp", None),
        P("grp", None),
        P("grp"),
        P("grp", None),
        P("grp", None),
        P("grp"),
    )
    return jax.shard_map(shards, mesh=mesh, in_specs=in_specs, out_specs=out_specs, check_vma=False)
```

```python
import functools

import jax
import jax.numpy as jnp
from jax import lax
from jax.experimental import pallas as pl
from jax.experimental.pallas import tpu as pltpu
from jax.sharding import PartitionSpec as P

AXES = ("dom", "sub", "feat")
SMEM = pl.BlockSpec(memory_space=pltpu.SMEM)
VMEM = pl.BlockSpec(memory_space=pltpu.VMEM)
VMEM_LIMIT = 8 * 2**20
F32 = jnp.float32
BF16 = jnp.bfloat16


def struct(shape, dtype):
    return jax.ShapeDtypeStruct(shape, dtype)


def swapped(value, mask):
    pairs = [(source, source ^ mask) for source in range(lax.axis_size(AXES))]
    return lax.ppermute(value, AXES, pairs)


def dot(a, b):
    return jnp.dot(a, b, preferred_element_type=F32)


def dot_bt(a, b):
    return lax.dot_general(a, b, (((1,), (1,)), ((), ())), preferred_element_type=F32)


def run(body, in_specs, out_specs, out_shape, scratch, args, flops=0, moved=0):
    return pl.pallas_call(
        body,
        in_specs=in_specs,
        out_specs=out_specs,
        out_shape=out_shape,
        scratch_shapes=scratch,
        compiler_params=pltpu.CompilerParams(vmem_limit_bytes=VMEM_LIMIT),
        cost_estimate=pl.CostEstimate(flops=flops, bytes_accessed=moved, transcendentals=0),
    )(*args)


class Table:
    def __init__(self, tiles, fan, rounds, slots):
        self.fan, self.slots = fan, slots
        self.where = tiles * fan
        self.dst = self.where + rounds * slots
        self.give = self.dst + rounds * slots
        self.size = self.give + rounds * slots

    def near_at(self, t, k):
        return t * self.fan + k

    def where_at(self, r, s):
        return self.where + r * self.slots + s

    def dst_at(self, r, s):
        return self.dst + r * self.slots + s

    def give_at(self, r, s):
        return self.give + r * self.slots + s


def stage_body(features, blocks, arrival):
    copy = pltpu.make_async_copy(features, blocks, arrival)
    copy.start()
    copy.wait()


def pick_body(rounds, *refs):
    partner_src = refs[:rounds]
    blocks = refs[rounds]
    outs = refs[rounds + 1 :]
    for r in range(rounds):
        row = partner_src[r][r]
        for s in range(outs[r].shape[0]):
            outs[r][s] = blocks[row[0, s]]


def first_local_body(
    at, rounds, index, dst, count, *refs
):
    partner_src = refs[:rounds]
    (features, values, edges, w1_self, bias, table, near, own, features_t, values_t,
     edges_t) = refs[rounds:]
    tiles, fan, size = values.shape[:3]
    slots = edges.shape[1]
    for t in range(tiles):
        for k in range(fan):
            table[at.near_at(t, k)] = index[k, t]
    for r in range(rounds):
        for s in range(slots):
            table[at.dst_at(r, s)] = dst[r, 0, s]
            table[at.where_at(r, s)] = jnp.where(s < count[0, r], dst[r, 0, s], tiles)
            table[at.give_at(r, s)] = partner_src[r][r, 0, s]
    for t in range(tiles):
        left = jnp.concatenate([values[t, k] for k in range(fan)], axis=1)
        right = jnp.concatenate([features[index[k, t]] for k in range(fan)], axis=0)
        near[t] = dot(left, right)
        own[t] = dot(features[t], w1_self[...]) + bias[...]
        features_t[:, t * size : (t + 1) * size] = features[t].T
        for k in range(fan):
            values_t[t, k] = values[t, k].T
    for r in range(rounds):
        for s in range(slots):
            live = s < count[0, r]
            edges_t[r, s] = jnp.where(live, edges[r, s].T, jnp.zeros_like(edges[r, s]))


def add_boundary(at, total, table, edges, arrived):
    rounds, slots = edges.shape[0], edges.shape[1]
    for r in range(rounds):
        for s in range(slots):
            where = table[at.where_at(r, s)]
            total[where] = total[where] + dot(edges[r, s], arrived[r][s])


def first_body(at, rounds, table, *refs):
    arrived = refs[:rounds]
    edges, near, own, w1_near, w2_near, first_agg, hidden, message = refs[rounds : rounds + 8]
    sends = refs[rounds + 8 : 2 * rounds + 8]
    total = refs[-1]
    tiles = near.shape[0]
    total[0:tiles] = near[...]
    add_boundary(at, total, table, edges, arrived)
    for t in range(tiles):
        agg = total[t].astype(BF16)
        first_agg[t] = agg
        pre = own[t] + dot(agg, w1_near[...])
        act = (pre * jax.nn.sigmoid(pre)).astype(BF16)
        hidden[t] = act
        message[t] = dot(act, w2_near[...]).astype(BF16)
    for r in range(rounds):
        for s in range(sends[r].shape[0]):
            sends[r][s] = message[table[at.give_at(r, s)]]


def second_local_body(
    at, table, labels, values, first_agg, own, hidden, message, w1_near, w2_self, bias,
    slope, near, target, first_agg_t, hidden_t,
):
    tiles, fan = values.shape[0], values.shape[1]
    classes = w2_self.shape[1]
    class_ids = lax.broadcasted_iota(jnp.int32, (classes, 128), 0)
    for t in range(tiles):
        left = jnp.concatenate([values[t, k] for k in range(fan)], axis=1)
        right = jnp.concatenate([message[table[at.near_at(t, k)]] for k in range(fan)], axis=0)
        near[t] = dot(left, right) + dot(hidden[t], w2_self[...]) + bias[...]
        hot = (labels[t : t + 1, :] == class_ids).astype(F32)
        target[t] = hot.T
        pre = own[t] + dot(first_agg[t], w1_near[...])
        sig = jax.nn.sigmoid(pre)
        slope[t] = sig * (1.0 + pre * (1.0 - sig))
        first_agg_t[:, t * 128 : (t + 1) * 128] = first_agg[t].T
        hidden_t[:, t * 128 : (t + 1) * 128] = hidden[t].T


def second_body(at, rounds, table, *refs):
    arrived = refs[:rounds]
    edges, edges_t, near, target, scores, error = refs[rounds : rounds + 6]
    sends = refs[rounds + 6 : 2 * rounds + 6]
    total = refs[-1]
    tiles = near.shape[0]
    total[0:tiles] = near[...]
    add_boundary(at, total, table, edges, arrived)
    for t in range(tiles):
        pre = total[t]
        scores[t] = pre.astype(BF16)
        error[t] = (pre - target[t]).astype(BF16)
    for r in range(rounds):
        for s in range(sends[r].shape[0]):
            sends[r][s] = dot(edges_t[r, s], error[table[at.dst_at(r, s)]]).astype(BF16)


def back_local_body(
    at, table, values_t, scores, error, hidden_t, w2_self,
    logits, back, self_grad, grad_w2_self, grad_bias_two,
):
    logits[...] = scores[...]
    tiles, fan = values_t.shape[0], values_t.shape[1]
    back[...] = jnp.zeros_like(back)
    bias = jnp.zeros((1, error.shape[2]), F32)
    for t in range(tiles):
        rows = error[t]
        for k in range(fan):
            where = table[at.near_at(t, k)]
            back[where] = back[where] + dot(values_t[t, k], rows)
        self_grad[t] = dot_bt(rows, w2_self[...])
        bias = bias + jnp.sum(rows.astype(F32), axis=0, keepdims=True)
    grad_bias_two[...] = bias
    flat = error[...].reshape(tiles * error.shape[1], error.shape[2])
    grad_w2_self[...] = dot(hidden_t[...], flat)


def back_body(at, rounds, table, *refs):
    arrived = refs[:rounds]
    (back, self_grad, slope, w2_near, features_t, first_agg_t, hidden_t, grad_w2_self, grad_bias_two,
     hidden_grad, send, keep, total, back_16, first_grad, packed) = refs[rounds:]
    tiles, size, classes = back.shape
    width = self_grad.shape[2]
    total[...] = back[...]
    for r in range(rounds):
        for s in range(arrived[r].shape[0]):
            where = table[at.give_at(r, s)]
            total[where] = total[where] + arrived[r][s].astype(F32)
    bias = jnp.zeros((1, width), F32)
    for t in range(tiles):
        here = slice(t * size, (t + 1) * size)
        rows = total[t].astype(BF16)
        back_16[here, :] = rows
        full = self_grad[t] + dot_bt(rows, w2_near[...])
        hidden_grad[t] = full.astype(BF16)
        grad = (full * slope[t]).astype(BF16)
        first_grad[here, :] = grad
        bias = bias + jnp.sum(grad.astype(F32), axis=0, keepdims=True)
    deep = features_t.shape[0]
    row = 0
    for left in (features_t, first_agg_t):
        product = dot(left[...], first_grad[...])
        for c in range(width // 128):
            packed[row : row + deep, :] = product[:, c * 128 : (c + 1) * 128]
            row += deep
    packed[row : row + width, :] = grad_w2_self[...]
    row += width
    packed[row : row + width, :] = dot(hidden_t[...], back_16[...])
    row += width
    packed[row:, :] = jnp.zeros_like(packed[row:, :])
    for c in range(width // 128):
        packed[row + c : row + c + 1, :] = bias[:, c * 128 : (c + 1) * 128]
    row += width // 128
    packed[row : row + 1, :] = grad_bias_two[...]
    half = keep.shape[0]
    mine = lax.axis_index("feat")
    keep[...] = packed[pl.ds(pl.multiple_of(mine * half, 16), half), :]
    send[...] = packed[pl.ds(pl.multiple_of((1 - mine) * half, 16), half), :].astype(BF16)


def leave_body(value, out):
    out[...] = value[...]


def spread_body(keep, arrived, own, *sends):
    rows = own.shape[0]
    for distance, out in enumerate((own, *sends)):
        owner = jnp.bitwise_xor(lax.axis_index("dom"), distance)
        here = pl.ds(pl.multiple_of(owner * rows, 16), rows)
        out[...] = (keep[here, :] + arrived[here, :].astype(F32)).astype(out.dtype)


def gather_body(own, *refs):
    total = own[...].astype(F32)
    for arrived in refs[:-1]:
        total = total + arrived[...].astype(F32)
    refs[-1][...] = total.astype(BF16)


def join_body(*refs):
    out = refs[-1]
    rows = refs[0].shape[0]
    for distance, piece in enumerate(refs[:-1]):
        owner = jnp.bitwise_xor(lax.axis_index("dom"), distance)
        out[pl.ds(pl.multiple_of(owner * rows, 16), rows), :] = piece[...]


def unpack_body(mine, other, g1_self, g1_near, g1_bias, g2_self, g2_near, g2_bias, packed):
    half = mine.shape[0]
    feat = lax.axis_index("feat")
    packed[pl.ds(pl.multiple_of(feat * half, 16), half), :] = mine[...].astype(F32)
    packed[pl.ds(pl.multiple_of((1 - feat) * half, 16), half), :] = other[...].astype(F32)
    deep, width = g1_self.shape
    row = 0
    for out in (g1_self, g1_near):
        for c in range(width // 128):
            out[:, c * 128 : (c + 1) * 128] = packed[row : row + deep, :]
            row += deep
    for out in (g2_self, g2_near):
        out[...] = packed[row : row + width, :]
        row += width
    for c in range(width // 128):
        g1_bias[:, c * 128 : (c + 1) * 128] = packed[row : row + 1, :]
        row += 1
    g2_bias[...] = packed[row : row + 1, :]


def shards(
    features,
    labels,
    local_index,
    local_values,
    cross_src,
    cross_dst,
    cross_count,
    cross_values,
    w1_self,
    w1_near,
    bias_one,
    w2_self,
    w2_near,
    bias_two,
):
    tiles, fan, size, _ = local_values.shape
    rounds, slots = cross_src.shape[1], cross_src.shape[2]
    width_in = features.shape[1]
    hidden_width = w1_self.shape[1]
    classes = w2_self.shape[1]
    nodes = tiles * size
    total_bits = lax.axis_size(AXES).bit_length() - 1
    masks = [1 << (total_bits - 1 - colour) for colour in range(rounds)]
    blocks = features.reshape(tiles, size, width_in)
    edges = cross_values[0]
    bias_one_row = bias_one.reshape(1, hidden_width)
    bias_two_row = bias_two.reshape(1, classes)
    label_rows = labels.reshape(tiles, size)

    at = Table(tiles, fan, rounds, slots)

    reads = cross_src.transpose(1, 0, 2)
    partner_src = [swapped(reads, mask) for mask in masks]
    blocks = run(
        stage_body,
        [pl.BlockSpec(memory_space=pltpu.HBM)],
        VMEM,
        struct(blocks.shape, BF16),
        [pltpu.SemaphoreType.DMA],
        [blocks],
        moved=2 * nodes * width_in * 2,
    )
    picks = run(
        functools.partial(pick_body, rounds),
        [VMEM] * rounds + [VMEM],
        [VMEM] * rounds,
        [struct((slots, size, width_in), BF16)] * rounds,
        [],
        [*partner_src, blocks],
        moved=2 * rounds * slots * size * width_in * 2,
    )
    arrived = [swapped(tile, mask) for tile, mask in zip(picks, masks)]

    table, near, own, features_t, values_t, edges_t = run(
        functools.partial(first_local_body, at, rounds),
        [SMEM] * (3 + rounds) + [VMEM] * 5,
        [SMEM] + [VMEM] * 5,
        [
            pltpu.SMEM((at.size,), jnp.int32),
            struct((tiles, size, width_in), F32),
            struct((tiles, size, hidden_width), F32),
            struct((width_in, nodes), BF16),
            struct(local_values.shape, BF16),
            struct(edges.shape, BF16),
        ],
        [],
        [
            local_index.T, cross_dst.transpose(1, 0, 2), cross_count, *partner_src,
            blocks, local_values, edges, w1_self, bias_one_row,
        ],
        flops=2 * nodes * width_in * (fan * size + hidden_width),
        moved=8 * 2**20,
    )

    first_agg, hidden, message, *sends = run(
        functools.partial(first_body, at, rounds),
        [SMEM] + [VMEM] * (rounds + 5),
        [VMEM] * (3 + rounds),
        [
            struct((tiles, size, width_in), BF16),
            struct((tiles, size, hidden_width), BF16),
            struct((tiles, size, classes), BF16),
        ]
        + [struct((slots, size, classes), BF16)] * rounds,
        [pltpu.VMEM((tiles + 1, size, width_in), F32)],
        [table, *arrived, edges, near, own, w1_near, w2_near],
        flops=2 * nodes * width_in * (rounds * slots * size // tiles + hidden_width + classes),
        moved=8 * 2**20,
    )
    arrived = [swapped(tile, mask) for tile, mask in zip(sends, masks)]

    slope, near, target, first_agg_t, hidden_t = run(
        functools.partial(second_local_body, at),
        [SMEM] + [VMEM] * 9,
        [VMEM] * 5,
        [
            struct((tiles, size, hidden_width), F32),
            struct((tiles, size, classes), F32),
            struct((tiles, size, classes), F32),
            struct((width_in, nodes), BF16),
            struct((hidden_width, nodes), BF16),
        ],
        [],
        [table, label_rows, local_values, first_agg, own, hidden, message, w1_near, w2_self, bias_two_row],
        flops=2 * nodes * classes * (fan * size + 3 * hidden_width),
        moved=6 * 2**20,
    )

    scores, error, *sends = run(
        functools.partial(second_body, at, rounds),
        [SMEM] + [VMEM] * (rounds + 4),
        [VMEM] * (2 + rounds),
        [struct((tiles, size, classes), BF16), struct((tiles, size, classes), BF16)]
        + [struct((slots, size, classes), BF16)] * rounds,
        [pltpu.VMEM((tiles + 1, size, classes), F32)],
        [table, *arrived, edges, edges_t, near, target],
        flops=4 * rounds * slots * size * size * classes,
        moved=3 * 2**20,
    )
    arrived = [swapped(tile, mask) for tile, mask in zip(sends, masks)]

    logits, back, self_grad, grad_w2_self, grad_bias_two = run(
        functools.partial(back_local_body, at),
        [SMEM] + [VMEM] * 5,
        [VMEM] * 5,
        [
            struct((tiles, size, classes), BF16),
            struct((tiles, size, classes), F32),
            struct((tiles, size, hidden_width), F32),
            struct((hidden_width, classes), F32),
            struct((1, classes), F32),
        ],
        [],
        [table, values_t, scores, error, hidden_t, w2_self],
        flops=2 * nodes * classes * (fan * size + 2 * hidden_width),
        moved=4 * 2**20,
    )

    lines, columns = lax.axis_size("dom"), lax.axis_size("sub")
    rows = (2 * width_in * hidden_width + 2 * hidden_width * classes + hidden_width + classes) // 128
    piece = -(-rows // (2 * lines * 16)) * 16
    half = piece * lines
    hidden_grad, send, keep = run(
        functools.partial(back_body, at, rounds),
        [SMEM] + [VMEM] * (rounds + 9),
        [VMEM] * 3,
        [
            struct((tiles, size, hidden_width), BF16),
            struct((half, 128), BF16),
            struct((half, 128), F32),
        ],
        [
            pltpu.VMEM((tiles, size, classes), F32),
            pltpu.VMEM((nodes, classes), BF16),
            pltpu.VMEM((nodes, hidden_width), BF16),
            pltpu.VMEM((2 * half, 128), F32),
        ],
        [
            table, *arrived, back, self_grad, slope, w2_near, features_t, first_agg_t,
            hidden_t, grad_w2_self, grad_bias_two,
        ],
        flops=2 * nodes * hidden_width * (2 * width_in + 2 * classes),
        moved=6 * 2**20,
    )

    arrived = swapped(send, 1)
    hidden_grad = run(
        leave_body, [VMEM], VMEM, struct(hidden_grad.shape, BF16), [],
        [hidden_grad], moved=4 * nodes * hidden_width,
    )

    along = [distance * 2 * columns for distance in range(1, lines)]
    piece_struct = struct((piece, 128), BF16)
    own, *sends = run(
        spread_body, [VMEM] * 2, [VMEM] * lines,
        [struct((piece, 128), F32)] + [piece_struct] * (lines - 1), [],
        [keep, arrived], flops=half * 128, moved=half * 128 * 8,
    )
    arrived = [swapped(value, mask) for value, mask in zip(sends, along)]
    total = run(
        gather_body, [VMEM] * lines, VMEM, piece_struct, [],
        [own, *arrived], flops=half * 128, moved=half * 128 * 2,
    )
    for bit in range(columns.bit_length() - 1):
        total = run(
            gather_body, [VMEM] * 2, VMEM, piece_struct, [],
            [total, swapped(total, 2 << bit)], flops=piece * 128, moved=piece * 128 * 6,
        )
    mine = run(
        join_body, [VMEM] * lines, VMEM, struct((half, 128), BF16), [],
        [total, *(swapped(total, mask) for mask in along)], moved=half * 128 * 4,
    )
    other = swapped(mine, 1)
    g1_self, g1_near, g1_bias, g2_self, g2_near, g2_bias = run(
        unpack_body,
        [VMEM] * 2,
        [VMEM] * 6,
        [
            struct((width_in, hidden_width), F32),
            struct((width_in, hidden_width), F32),
            struct((1, hidden_width), F32),
            struct((hidden_width, classes), F32),
            struct((hidden_width, classes), F32),
            struct((1, classes), F32),
        ],
        [pltpu.VMEM((2 * half, 128), F32)],
        [mine, other],
        moved=half * 128 * 12,
    )
    return (
        logits.reshape(nodes, classes),
        hidden_grad.reshape(nodes, hidden_width),
        g1_self,
        g1_near,
        g1_bias.reshape(hidden_width),
        g2_self,
        g2_near,
        g2_bias.reshape(classes),
    )


def solution(mesh):
    in_specs = (
        P(("grp", "dom", "sub", "feat"), None),
        P(("grp", "dom", "sub", "feat")),
        P(("grp", "dom", "sub", "feat"), None),
        P(("grp", "dom", "sub", "feat"), None, None, None),
        P(("grp", "dom", "sub", "feat"), None, None),
        P(("grp", "dom", "sub", "feat"), None, None),
        P(("grp", "dom", "sub", "feat"), None),
        P(("grp", "dom", "sub", "feat"), None, None, None, None),
        P(),
        P(),
        P(),
        P(),
        P(),
        P(),
    )
    out_specs = (
        P(("grp", "dom", "sub", "feat"), None),
        P(("grp", "dom", "sub", "feat"), None),
        P("grp", None),
        P("grp", None),
        P("grp"),
        P("grp", None),
        P("grp", None),
        P("grp"),
    )
    return jax.shard_map(shards, mesh=mesh, in_specs=in_specs, out_specs=out_specs, check_vma=False)
```

```python
import functools

import jax
import jax.numpy as jnp
from jax import lax
from jax.experimental import pallas as pl
from jax.experimental.pallas import tpu as pltpu
from jax.sharding import PartitionSpec as P

AXES = ("dom", "sub", "feat")
SMEM = pl.BlockSpec(memory_space=pltpu.SMEM)
VMEM = pl.BlockSpec(memory_space=pltpu.VMEM)
HBM = pl.BlockSpec(memory_space=pltpu.HBM)
VMEM_LIMIT = 8 * 2**20
F32 = jnp.float32
BF16 = jnp.bfloat16


def struct(shape, dtype):
    return jax.ShapeDtypeStruct(shape, dtype)


def swapped(value, mask):
    pairs = [(source, source ^ mask) for source in range(lax.axis_size(AXES))]
    return lax.ppermute(value, AXES, pairs)


def dot(a, b):
    return jnp.dot(a, b, preferred_element_type=F32)


def dot_bt(a, b):
    return lax.dot_general(a, b, (((1,), (1,)), ((), ())), preferred_element_type=F32)


def run(body, in_specs, out_specs, out_shape, scratch, args, flops=0, moved=0, aliases=()):
    return pl.pallas_call(
        body,
        in_specs=in_specs,
        out_specs=out_specs,
        out_shape=out_shape,
        scratch_shapes=scratch,
        input_output_aliases=dict(aliases),
        compiler_params=pltpu.CompilerParams(vmem_limit_bytes=VMEM_LIMIT),
        cost_estimate=pl.CostEstimate(flops=flops, bytes_accessed=moved, transcendentals=0),
    )(*args)


class Table:
    def __init__(self, tiles, fan, rounds, slots):
        self.fan, self.slots = fan, slots
        self.where = tiles * fan
        self.dst = self.where + rounds * slots
        self.give = self.dst + rounds * slots
        self.size = self.give + rounds * slots

    def near_at(self, t, k):
        return t * self.fan + k

    def where_at(self, r, s):
        return self.where + r * self.slots + s

    def dst_at(self, r, s):
        return self.dst + r * self.slots + s

    def give_at(self, r, s):
        return self.give + r * self.slots + s


def stage_body(features, blocks, arrival):
    copy = pltpu.make_async_copy(features, blocks, arrival)
    copy.start()
    copy.wait()


def pick_body(rounds, *refs):
    partner_src = refs[:rounds]
    blocks = refs[rounds]
    outs = refs[rounds + 1 :]
    for r in range(rounds):
        row = partner_src[r][r]
        for s in range(outs[r].shape[0]):
            outs[r][s] = blocks[row[0, s]]


def first_local_body(
    at, rounds, index, dst, count, *refs
):
    partner_src = refs[:rounds]
    (features, values, edges, w1_self, bias, table, near, own, features_t, values_t,
     edges_t) = refs[rounds:]
    tiles, fan, size = values.shape[:3]
    slots = edges.shape[1]
    for t in range(tiles):
        for k in range(fan):
            table[at.near_at(t, k)] = index[k, t]
    for r in range(rounds):
        for s in range(slots):
            table[at.dst_at(r, s)] = dst[r, 0, s]
            table[at.where_at(r, s)] = jnp.where(s < count[0, r], dst[r, 0, s], tiles)
            table[at.give_at(r, s)] = partner_src[r][r, 0, s]
    for t in range(tiles):
        left = jnp.concatenate([values[t, k] for k in range(fan)], axis=1)
        right = jnp.concatenate([features[index[k, t]] for k in range(fan)], axis=0)
        near[t] = dot(left, right)
        own[t] = dot(features[t], w1_self[...]) + bias[...]
        features_t[:, t * size : (t + 1) * size] = features[t].T
        for k in range(fan):
            values_t[t, k] = values[t, k].T
    for r in range(rounds):
        for s in range(slots):
            live = s < count[0, r]
            edges_t[r, s] = jnp.where(live, edges[r, s].T, jnp.zeros_like(edges[r, s]))


def add_boundary(at, total, table, edges, arrived):
    rounds, slots = edges.shape[0], edges.shape[1]
    for r in range(rounds):
        for s in range(slots):
            where = table[at.where_at(r, s)]
            total[where] = total[where] + dot(edges[r, s], arrived[r][s])


def first_body(at, rounds, table, *refs):
    arrived = refs[:rounds]
    edges, near, own, w1_near, w2_near, first_agg, hidden, message = refs[rounds : rounds + 8]
    sends = refs[rounds + 8 : 2 * rounds + 8]
    total = refs[-1]
    tiles = near.shape[0]
    total[0:tiles] = near[...]
    add_boundary(at, total, table, edges, arrived)
    for t in range(tiles):
        agg = total[t].astype(BF16)
        first_agg[t] = agg
        pre = own[t] + dot(agg, w1_near[...])
        act = (pre * jax.nn.sigmoid(pre)).astype(BF16)
        hidden[t] = act
        message[t] = dot(act, w2_near[...]).astype(BF16)
    for r in range(rounds):
        for s in range(sends[r].shape[0]):
            sends[r][s] = message[table[at.give_at(r, s)]]


def second_local_body(
    at, table, labels, values, first_agg, own, hidden, message, w1_near, w2_self, bias,
    slope, near, target, first_agg_t, hidden_t,
):
    tiles, fan = values.shape[0], values.shape[1]
    classes = w2_self.shape[1]
    class_ids = lax.broadcasted_iota(jnp.int32, (classes, 128), 0)
    for t in range(tiles):
        left = jnp.concatenate([values[t, k] for k in range(fan)], axis=1)
        right = jnp.concatenate([message[table[at.near_at(t, k)]] for k in range(fan)], axis=0)
        near[t] = dot(left, right) + dot(hidden[t], w2_self[...]) + bias[...]
        hot = (labels[t : t + 1, :] == class_ids).astype(F32)
        target[t] = hot.T
        pre = own[t] + dot(first_agg[t], w1_near[...])
        sig = jax.nn.sigmoid(pre)
        slope[t] = sig * (1.0 + pre * (1.0 - sig))
        first_agg_t[:, t * 128 : (t + 1) * 128] = first_agg[t].T
        hidden_t[:, t * 128 : (t + 1) * 128] = hidden[t].T


def second_body(at, rounds, table, *refs):
    arrived = refs[:rounds]
    edges, edges_t, near, target, scores, error = refs[rounds : rounds + 6]
    sends = refs[rounds + 6 : 2 * rounds + 6]
    total = refs[-1]
    tiles = near.shape[0]
    total[0:tiles] = near[...]
    add_boundary(at, total, table, edges, arrived)
    for t in range(tiles):
        pre = total[t]
        scores[t] = pre.astype(BF16)
        error[t] = (pre - target[t]).astype(BF16)
    for r in range(rounds):
        for s in range(sends[r].shape[0]):
            sends[r][s] = dot(edges_t[r, s], error[table[at.dst_at(r, s)]]).astype(BF16)


def back_local_body(
    at, table, values_t, scores, error, hidden_t, w2_self,
    logits, back, self_grad, grad_w2_self, grad_bias_two,
):
    logits[...] = scores[...]
    tiles, fan = values_t.shape[0], values_t.shape[1]
    back[...] = jnp.zeros_like(back)
    bias = jnp.zeros((1, error.shape[2]), F32)
    for t in range(tiles):
        rows = error[t]
        for k in range(fan):
            where = table[at.near_at(t, k)]
            back[where] = back[where] + dot(values_t[t, k], rows)
        self_grad[t] = dot_bt(rows, w2_self[...])
        bias = bias + jnp.sum(rows.astype(F32), axis=0, keepdims=True)
    grad_bias_two[...] = bias
    flat = error[...].reshape(tiles * error.shape[1], error.shape[2])
    grad_w2_self[...] = dot(hidden_t[...], flat)


def back_body(at, rounds, table, *refs):
    arrived = refs[:rounds]
    (back, self_grad, slope, w2_near, features_t, first_agg_t, hidden_t, grad_w2_self, grad_bias_two,
     hidden_grad, send, keep, total, back_16, first_grad, packed) = refs[rounds:]
    tiles, size, classes = back.shape
    width = self_grad.shape[2]
    total[...] = back[...]
    for r in range(rounds):
        for s in range(arrived[r].shape[0]):
            where = table[at.give_at(r, s)]
            total[where] = total[where] + arrived[r][s].astype(F32)
    bias = jnp.zeros((1, width), F32)
    for t in range(tiles):
        here = slice(t * size, (t + 1) * size)
        rows = total[t].astype(BF16)
        back_16[here, :] = rows
        full = self_grad[t] + dot_bt(rows, w2_near[...])
        hidden_grad[t] = full.astype(BF16)
        grad = (full * slope[t]).astype(BF16)
        first_grad[here, :] = grad
        bias = bias + jnp.sum(grad.astype(F32), axis=0, keepdims=True)
    blocks = []
    for left in (features_t, first_agg_t):
        product = dot(left[...], first_grad[...])
        blocks += [product[:, c * 128 : (c + 1) * 128] for c in range(width // 128)]
    blocks += [grad_w2_self[...], dot(hidden_t[...], back_16[...])]
    row = 0
    for block in blocks:
        deep = block.shape[0] // 2
        for h in range(2):
            packed[h, row : row + deep, :] = block[h * deep : (h + 1) * deep, :]
        row += deep
    packed[:, row:, :] = jnp.zeros_like(packed[:, row:, :])
    for c in range(width // 128):
        packed[0, row + c : row + c + 1, :] = bias[:, c * 128 : (c + 1) * 128]
    row += width // 128
    packed[0, row : row + 1, :] = grad_bias_two[...]
    mine = lax.axis_index("feat")
    lines, piece = keep.shape[:2]
    for line in range(lines):
        here = slice(line * piece, (line + 1) * piece)
        keep[line] = packed[mine, here, :]
        send[line] = packed[1 - mine, here, :].astype(BF16)


def leave_body(value, out):
    out[...] = value[...]


def spread_body(keep, arrived, own, *sends):
    for distance, out in enumerate((own, *sends)):
        owner = jnp.bitwise_xor(lax.axis_index("dom"), distance)
        out[...] = (keep[owner] + arrived[owner].astype(F32)).astype(out.dtype)


def gather_body(own, *refs):
    total = own[...].astype(F32)
    for arrived in refs[:-1]:
        total = total + arrived[...].astype(F32)
    refs[-1][...] = total.astype(BF16)


def join_body(*refs):
    for distance, piece in enumerate(refs[:-1]):
        refs[-1][jnp.bitwise_xor(lax.axis_index("dom"), distance)] = piece[...]


def place_half(h, value, outs, stages, sems):
    copies, row = [], 0
    for out, stage in zip(outs, stages):
        deep, width = stage.shape
        for c in range(width // 128):
            stage[:, c * 128 : (c + 1) * 128] = value[row : row + deep, :]
            row += deep
        there = out.at[pl.ds(pl.multiple_of(h * deep, 8), deep), :]
        copies.append(pltpu.make_async_copy(stage, there, sems.at[len(copies)]))
        copies[-1].start()
    return copies


def unpack_mine_body(turned, mine, *refs):
    count = (len(refs) - 1) // 2
    value = mine[...].astype(F32).reshape(-1, 128)
    half = jnp.bitwise_xor(lax.axis_index("feat"), turned)
    for copy in place_half(half, value, refs[:count], refs[count:-1], refs[-1]):
        copy.wait()


def unpack_other_body(turned, mine, other, *refs):
    count = (len(refs) - 5) // 3
    outs, biases = refs[count : 2 * count], refs[2 * count : 2 * count + 2]
    stages, bias_stages = refs[2 * count + 2 : 3 * count + 2], refs[3 * count + 2 : 3 * count + 4]
    half = jnp.bitwise_xor(lax.axis_index("feat"), turned)
    value = other[...].astype(F32).reshape(-1, 128)
    copies = place_half(1 - half, value, outs, stages, refs[-1])
    rest = jnp.where(half == 0, mine[...].astype(F32).reshape(-1, 128), value)
    row = sum(stage.shape[0] * (stage.shape[1] // 128) for stage in stages)
    for out, stage in zip(biases, bias_stages):
        for c in range(stage.shape[1] // 128):
            stage[:, c * 128 : (c + 1) * 128] = rest[row : row + 1, :]
            row += 1
        copies.append(pltpu.make_async_copy(stage, out, refs[-1].at[len(copies)]))
        copies[-1].start()
    for copy in copies:
        copy.wait()


def shards(
    features,
    labels,
    local_index,
    local_values,
    cross_src,
    cross_dst,
    cross_count,
    cross_values,
    w1_self,
    w1_near,
    bias_one,
    w2_self,
    w2_near,
    bias_two,
):
    tiles, fan, size, _ = local_values.shape
    rounds, slots = cross_src.shape[1], cross_src.shape[2]
    width_in = features.shape[1]
    hidden_width = w1_self.shape[1]
    classes = w2_self.shape[1]
    nodes = tiles * size
    total_bits = lax.axis_size(AXES).bit_length() - 1
    masks = [1 << (total_bits - 1 - colour) for colour in range(rounds)]
    blocks = features.reshape(tiles, size, width_in)
    edges = cross_values[0]
    bias_one_row = bias_one.reshape(1, hidden_width)
    bias_two_row = bias_two.reshape(1, classes)
    label_rows = labels.reshape(tiles, size)

    at = Table(tiles, fan, rounds, slots)

    reads = cross_src.transpose(1, 0, 2)
    partner_src = [swapped(reads, mask) for mask in masks]
    blocks = run(
        stage_body,
        [HBM],
        VMEM,
        struct(blocks.shape, BF16),
        [pltpu.SemaphoreType.DMA],
        [blocks],
        moved=2 * nodes * width_in * 2,
    )
    picks = run(
        functools.partial(pick_body, rounds),
        [VMEM] * rounds + [VMEM],
        [VMEM] * rounds,
        [struct((slots, size, width_in), BF16)] * rounds,
        [],
        [*partner_src, blocks],
        moved=2 * rounds * slots * size * width_in * 2,
    )
    arrived = [swapped(tile, mask) for tile, mask in zip(picks, masks)]

    table, near, own, features_t, values_t, edges_t = run(
        functools.partial(first_local_body, at, rounds),
        [SMEM] * (3 + rounds) + [VMEM] * 5,
        [SMEM] + [VMEM] * 5,
        [
            pltpu.SMEM((at.size,), jnp.int32),
            struct((tiles, size, width_in), F32),
            struct((tiles, size, hidden_width), F32),
            struct((width_in, nodes), BF16),
            struct(local_values.shape, BF16),
            struct(edges.shape, BF16),
        ],
        [],
        [
            local_index.T, cross_dst.transpose(1, 0, 2), cross_count, *partner_src,
            blocks, local_values, edges, w1_self, bias_one_row,
        ],
        flops=2 * nodes * width_in * (fan * size + hidden_width),
        moved=8 * 2**20,
    )

    first_agg, hidden, message, *sends = run(
        functools.partial(first_body, at, rounds),
        [SMEM] + [VMEM] * (rounds + 5),
        [VMEM] * (3 + rounds),
        [
            struct((tiles, size, width_in), BF16),
            struct((tiles, size, hidden_width), BF16),
            struct((tiles, size, classes), BF16),
        ]
        + [struct((slots, size, classes), BF16)] * rounds,
        [pltpu.VMEM((tiles + 1, size, width_in), F32)],
        [table, *arrived, edges, near, own, w1_near, w2_near],
        flops=2 * nodes * width_in * (rounds * slots * size // tiles + hidden_width + classes),
        moved=8 * 2**20,
    )
    arrived = [swapped(tile, mask) for tile, mask in zip(sends, masks)]

    slope, near, target, first_agg_t, hidden_t = run(
        functools.partial(second_local_body, at),
        [SMEM] + [VMEM] * 9,
        [VMEM] * 5,
        [
            struct((tiles, size, hidden_width), F32),
            struct((tiles, size, classes), F32),
            struct((tiles, size, classes), F32),
            struct((width_in, nodes), BF16),
            struct((hidden_width, nodes), BF16),
        ],
        [],
        [table, label_rows, local_values, first_agg, own, hidden, message, w1_near, w2_self, bias_two_row],
        flops=2 * nodes * classes * (fan * size + 3 * hidden_width),
        moved=6 * 2**20,
    )

    scores, error, *sends = run(
        functools.partial(second_body, at, rounds),
        [SMEM] + [VMEM] * (rounds + 4),
        [VMEM] * (2 + rounds),
        [struct((tiles, size, classes), BF16), struct((tiles, size, classes), BF16)]
        + [struct((slots, size, classes), BF16)] * rounds,
        [pltpu.VMEM((tiles + 1, size, classes), F32)],
        [table, *arrived, edges, edges_t, near, target],
        flops=4 * rounds * slots * size * size * classes,
        moved=3 * 2**20,
    )
    arrived = [swapped(tile, mask) for tile, mask in zip(sends, masks)]

    logits, back, self_grad, grad_w2_self, grad_bias_two = run(
        functools.partial(back_local_body, at),
        [SMEM] + [VMEM] * 5,
        [VMEM] * 5,
        [
            struct((tiles, size, classes), BF16),
            struct((tiles, size, classes), F32),
            struct((tiles, size, hidden_width), F32),
            struct((hidden_width, classes), F32),
            struct((1, classes), F32),
        ],
        [],
        [table, values_t, scores, error, hidden_t, w2_self],
        flops=2 * nodes * classes * (fan * size + 2 * hidden_width),
        moved=4 * 2**20,
    )

    lines, columns = lax.axis_size("dom"), lax.axis_size("sub")
    lines, columns = lax.axis_size("dom"), lax.axis_size("sub")
    matrices = [(width_in, hidden_width)] * 2 + [(hidden_width, classes)] * 2
    rows = sum(deep * width // 256 for deep, width in matrices) + (hidden_width + classes) // 128
    piece = -(-rows // (lines * 8)) * 8
    half = (lines, piece, 128)
    hidden_grad, send, keep = run(
        functools.partial(back_body, at, rounds),
        [SMEM] + [VMEM] * (rounds + 9),
        [VMEM] * 3,
        [
            struct((tiles, size, hidden_width), BF16),
            struct(half, BF16),
            struct(half, F32),
        ],
        [
            pltpu.VMEM((tiles, size, classes), F32),
            pltpu.VMEM((nodes, classes), BF16),
            pltpu.VMEM((nodes, hidden_width), BF16),
            pltpu.VMEM((2, lines * piece, 128), F32),
        ],
        [
            table, *arrived, back, self_grad, slope, w2_near, features_t, first_agg_t,
            hidden_t, grad_w2_self, grad_bias_two,
        ],
        flops=2 * nodes * hidden_width * (2 * width_in + 2 * classes),
        moved=6 * 2**20,
    )

    arrived = swapped(send, 1)
    hidden_grad = run(
        leave_body, [VMEM], VMEM, struct(hidden_grad.shape, BF16), [],
        [hidden_grad], moved=4 * nodes * hidden_width,
    )
    arrived, hidden_grad = lax.optimization_barrier((arrived, hidden_grad))

    along = [distance * 2 * columns for distance in range(1, lines)]
    piece_struct = struct((piece, 128), BF16)
    own, *sends = run(
        spread_body, [VMEM] * 2, [VMEM] * lines,
        [struct((piece, 128), F32)] + [piece_struct] * (lines - 1), [],
        [keep, arrived], flops=lines * piece * 128, moved=lines * piece * 128 * 8,
    )
    arrived = [swapped(value, mask) for value, mask in zip(sends, along)]
    total = run(
        gather_body, [VMEM] * lines, VMEM, piece_struct, [],
        [own, *arrived], flops=lines * piece * 128, moved=lines * piece * 128 * 2,
    )
    turned = (columns.bit_length() - 1) % 2
    for bit in range(columns.bit_length() - 1):
        total = run(
            gather_body, [VMEM] * 2, VMEM, piece_struct, [],
            [swapped(total, 1), swapped(total, (2 << bit) | 1)], flops=piece * 128, moved=piece * 128 * 6,
        )
    mine = run(
        join_body, [VMEM] * lines, VMEM, struct(half, BF16), [],
        [total, *(swapped(total, mask) for mask in along)], moved=lines * piece * 128 * 4,
    )
    other = swapped(mine, 1)
    stages = [pltpu.VMEM((deep // 2, width), F32) for deep, width in matrices]
    sems = pltpu.SemaphoreType.DMA((len(matrices) + 2,))
    biases = [(1, hidden_width), (1, classes)]
    outs = [struct(shape, F32) for shape in matrices]
    halves = run(
        functools.partial(unpack_mine_body, turned), [VMEM], [HBM] * len(outs), outs, [*stages, sems],
        [mine], moved=lines * piece * 128 * 6,
    )
    g1_self, g1_near, g2_self, g2_near, g1_bias, g2_bias = run(
        functools.partial(unpack_other_body, turned),
        [VMEM] * 2 + [HBM] * len(outs),
        [HBM] * (len(outs) + 2),
        outs + [struct(shape, F32) for shape in biases],
        [*stages, *[pltpu.VMEM(shape, F32) for shape in biases], sems],
        [mine, other, *halves],
        moved=lines * piece * 128 * 6,
        aliases={2 + n: n for n in range(len(outs))},
    )
    return (
        logits.reshape(nodes, classes),
        hidden_grad.reshape(nodes, hidden_width),
        g1_self,
        g1_near,
        g1_bias.reshape(hidden_width),
        g2_self,
        g2_near,
        g2_bias.reshape(classes),
    )


def solution(mesh):
    in_specs = (
        P(("grp", "dom", "sub", "feat"), None),
        P(("grp", "dom", "sub", "feat")),
        P(("grp", "dom", "sub", "feat"), None),
        P(("grp", "dom", "sub", "feat"), None, None, None),
        P(("grp", "dom", "sub", "feat"), None, None),
        P(("grp", "dom", "sub", "feat"), None, None),
        P(("grp", "dom", "sub", "feat"), None),
        P(("grp", "dom", "sub", "feat"), None, None, None, None),
        P(),
        P(),
        P(),
        P(),
        P(),
        P(),
    )
    out_specs = (
        P(("grp", "dom", "sub", "feat"), None),
        P(("grp", "dom", "sub", "feat"), None),
        P("grp", None),
        P("grp", None),
        P("grp"),
        P("grp", None),
        P("grp", None),
        P("grp"),
    )
    return jax.shard_map(shards, mesh=mesh, in_specs=in_specs, out_specs=out_specs, check_vma=False)
```

```python
import functools

import jax
import jax.numpy as jnp
from jax import lax
from jax.experimental import pallas as pl
from jax.experimental.pallas import tpu as pltpu
from jax.sharding import PartitionSpec as P

AXES = ("dom", "sub", "feat")
SMEM = pl.BlockSpec(memory_space=pltpu.SMEM)
VMEM = pl.BlockSpec(memory_space=pltpu.VMEM)
HBM = pl.BlockSpec(memory_space=pltpu.HBM)
VMEM_LIMIT = 8 * 2**20
F32 = jnp.float32
BF16 = jnp.bfloat16


def struct(shape, dtype):
    return jax.ShapeDtypeStruct(shape, dtype)


def swapped(value, mask):
    pairs = [(source, source ^ mask) for source in range(lax.axis_size(AXES))]
    return lax.ppermute(value, AXES, pairs)


def dot(a, b):
    return jnp.dot(a, b, preferred_element_type=F32)


def dot_bt(a, b):
    return lax.dot_general(a, b, (((1,), (1,)), ((), ())), preferred_element_type=F32)


def run(body, in_specs, out_specs, out_shape, scratch, args, flops=0, moved=0, aliases=()):
    return pl.pallas_call(
        body,
        in_specs=in_specs,
        out_specs=out_specs,
        out_shape=out_shape,
        scratch_shapes=scratch,
        input_output_aliases=dict(aliases),
        compiler_params=pltpu.CompilerParams(vmem_limit_bytes=VMEM_LIMIT),
        cost_estimate=pl.CostEstimate(flops=flops, bytes_accessed=moved, transcendentals=0),
    )(*args)


class Table:
    def __init__(self, tiles, fan, rounds, slots):
        self.fan, self.slots = fan, slots
        self.where = tiles * fan
        self.dst = self.where + rounds * slots
        self.give = self.dst + rounds * slots
        self.size = self.give + rounds * slots

    def near_at(self, t, k):
        return t * self.fan + k

    def where_at(self, r, s):
        return self.where + r * self.slots + s

    def dst_at(self, r, s):
        return self.dst + r * self.slots + s

    def give_at(self, r, s):
        return self.give + r * self.slots + s


def stage_body(features, blocks, arrival):
    copy = pltpu.make_async_copy(features, blocks, arrival)
    copy.start()
    copy.wait()


def pick_body(rounds, *refs):
    partner_src = refs[:rounds]
    blocks = refs[rounds]
    outs = refs[rounds + 1 :]
    for r in range(rounds):
        row = partner_src[r][r]
        for s in range(outs[r].shape[0]):
            outs[r][s] = blocks[row[0, s]]


def first_local_body(
    at, rounds, index, dst, count, *refs
):
    partner_src = refs[:rounds]
    (features, values, edges, w1_self, bias, table, near, own, features_t, values_t,
     edges_t) = refs[rounds:]
    tiles, fan, size = values.shape[:3]
    slots = edges.shape[1]
    for t in range(tiles):
        for k in range(fan):
            table[at.near_at(t, k)] = index[k, t]
    for r in range(rounds):
        for s in range(slots):
            table[at.dst_at(r, s)] = dst[r, 0, s]
            table[at.where_at(r, s)] = jnp.where(s < count[0, r], dst[r, 0, s], tiles)
            table[at.give_at(r, s)] = partner_src[r][r, 0, s]
    for t in range(tiles):
        left = jnp.concatenate([values[t, k] for k in range(fan)], axis=1)
        right = jnp.concatenate([features[index[k, t]] for k in range(fan)], axis=0)
        near[t] = dot(left, right)
        own[t] = dot(features[t], w1_self[...]) + bias[...]
        features_t[:-16, t * size : (t + 1) * size] = features[t].T
        for k in range(fan):
            values_t[t, k] = values[t, k].T
    features_t[-16:, :] = jnp.ones_like(features_t[-16:, :])
    for r in range(rounds):
        for s in range(slots):
            live = s < count[0, r]
            edges_t[r, s] = jnp.where(live, edges[r, s].T, jnp.zeros_like(edges[r, s]))


def add_boundary(at, total, table, edges, arrived):
    rounds, slots = edges.shape[0], edges.shape[1]
    for r in range(rounds):
        for s in range(slots):
            where = table[at.where_at(r, s)]
            total[where] = total[where] + dot(edges[r, s], arrived[r][s])


def first_body(at, rounds, table, *refs):
    arrived = refs[:rounds]
    edges, near, own, w1_near, w2_near, first_agg, hidden, message = refs[rounds : rounds + 8]
    sends = refs[rounds + 8 : 2 * rounds + 8]
    total = refs[-1]
    tiles = near.shape[0]
    total[0:tiles] = near[...]
    add_boundary(at, total, table, edges, arrived)
    for t in range(tiles):
        agg = total[t].astype(BF16)
        first_agg[t] = agg
        pre = own[t] + dot(agg, w1_near[...])
        act = (pre * jax.nn.sigmoid(pre)).astype(BF16)
        hidden[t] = act
        message[t] = dot(act, w2_near[...]).astype(BF16)
    for r in range(rounds):
        for s in range(sends[r].shape[0]):
            sends[r][s] = message[table[at.give_at(r, s)]]


def second_local_body(
    at, table, labels, values, first_agg, own, hidden, message, w1_near, w2_self, bias,
    slope, near, target, first_agg_t, hidden_t,
):
    tiles, fan = values.shape[0], values.shape[1]
    classes = w2_self.shape[1]
    class_ids = lax.broadcasted_iota(jnp.int32, (classes, 128), 0)
    for t in range(tiles):
        left = jnp.concatenate([values[t, k] for k in range(fan)], axis=1)
        right = jnp.concatenate([message[table[at.near_at(t, k)]] for k in range(fan)], axis=0)
        near[t] = dot(left, right) + dot(hidden[t], w2_self[...]) + bias[...]
        hot = (labels[t : t + 1, :] == class_ids).astype(F32)
        target[t] = hot.T
        pre = own[t] + dot(first_agg[t], w1_near[...])
        sig = jax.nn.sigmoid(pre)
        slope[t] = sig * (1.0 + pre * (1.0 - sig))
        first_agg_t[:, t * 128 : (t + 1) * 128] = first_agg[t].T
        hidden_t[:, t * 128 : (t + 1) * 128] = hidden[t].T


def second_body(at, rounds, table, *refs):
    arrived = refs[:rounds]
    edges, edges_t, near, target, scores, error = refs[rounds : rounds + 6]
    sends = refs[rounds + 6 : 2 * rounds + 6]
    total = refs[-1]
    tiles = near.shape[0]
    total[0:tiles] = near[...]
    add_boundary(at, total, table, edges, arrived)
    for t in range(tiles):
        pre = total[t]
        scores[t] = pre.astype(BF16)
        error[t] = (pre - target[t]).astype(BF16)
    for r in range(rounds):
        for s in range(sends[r].shape[0]):
            sends[r][s] = dot(edges_t[r, s], error[table[at.dst_at(r, s)]]).astype(BF16)


def back_local_body(
    at, table, values_t, scores, error, hidden_t, w2_self,
    logits, back, self_grad, grad_w2_self, grad_bias_two,
):
    logits[...] = scores[...]
    tiles, fan = values_t.shape[0], values_t.shape[1]
    back[...] = jnp.zeros_like(back)
    bias = jnp.zeros((1, error.shape[2]), F32)
    for t in range(tiles):
        rows = error[t]
        for k in range(fan):
            where = table[at.near_at(t, k)]
            back[where] = back[where] + dot(values_t[t, k], rows)
        self_grad[t] = dot_bt(rows, w2_self[...])
        bias = bias + jnp.sum(rows.astype(F32), axis=0, keepdims=True)
    grad_bias_two[...] = bias
    flat = error[...].reshape(tiles * error.shape[1], error.shape[2])
    grad_w2_self[...] = dot(hidden_t[...], flat)


def back_body(at, rounds, table, *refs):
    arrived = refs[:rounds]
    (back, self_grad, slope, w2_near, features_t, first_agg_t, hidden_t, grad_w2_self, grad_bias_two,
     hidden_grad, send, keep, total, back_16, first_grad, packed) = refs[rounds:]
    tiles, size, classes = back.shape
    width = self_grad.shape[2]
    total[...] = back[...]
    for r in range(rounds):
        for s in range(arrived[r].shape[0]):
            where = table[at.give_at(r, s)]
            total[where] = total[where] + arrived[r][s].astype(F32)
    for t in range(tiles):
        here = slice(t * size, (t + 1) * size)
        rows = total[t].astype(BF16)
        back_16[here, :] = rows
        full = self_grad[t] + dot_bt(rows, w2_near[...])
        hidden_grad[t] = full.astype(BF16)
        grad = (full * slope[t]).astype(BF16)
        first_grad[here, :] = grad
    blocks = []
    width_in = first_agg_t.shape[0]
    for left in (features_t, first_agg_t):
        product = dot(left[...], first_grad[...])
        if left is features_t:
            bias = product[width_in : width_in + 1, :]
        blocks += [product[:width_in, c * 128 : (c + 1) * 128] for c in range(width // 128)]
    blocks += [grad_w2_self[...], dot(hidden_t[...], back_16[...])]
    row = 0
    for block in blocks:
        deep = block.shape[0] // 2
        for h in range(2):
            packed[h, row : row + deep, :] = block[h * deep : (h + 1) * deep, :]
        row += deep
    packed[:, row:, :] = jnp.zeros_like(packed[:, row:, :])
    for c in range(width // 128):
        packed[0, row + c : row + c + 1, :] = bias[:, c * 128 : (c + 1) * 128]
    row += width // 128
    packed[0, row : row + 1, :] = grad_bias_two[...]
    mine = lax.axis_index("feat")
    lines, piece = keep.shape[:2]
    for line in range(lines):
        here = slice(line * piece, (line + 1) * piece)
        keep[line] = packed[mine, here, :]
        send[line] = packed[1 - mine, here, :].astype(BF16)


def leave_body(value, out):
    out[...] = value[...]


def spread_body(keep, arrived, own, *sends):
    for distance, out in enumerate((own, *sends)):
        owner = jnp.bitwise_xor(lax.axis_index("dom"), distance)
        out[...] = (keep[owner] + arrived[owner].astype(F32)).astype(out.dtype)


def gather_body(own, *refs):
    total = own[...].astype(F32)
    for arrived in refs[:-1]:
        total = total + arrived[...].astype(F32)
    refs[-1][...] = total.astype(BF16)


def in_order(distances, pieces, held):
    for distance, piece in zip(distances, pieces):
        held[jnp.bitwise_xor(lax.axis_index("dom"), distance)] = piece[...].astype(F32)
    return held[...].reshape(-1, 128)


def place_half(h, value, outs, stages, sems):
    copies, row = [], 0
    for out, stage in zip(outs, stages):
        deep, width = stage.shape
        for c in range(width // 128):
            stage[:, c * 128 : (c + 1) * 128] = value[row : row + deep, :]
            row += deep
        there = out.at[pl.ds(pl.multiple_of(h * deep, 8), deep), :]
        copies.append(pltpu.make_async_copy(stage, there, sems.at[len(copies)]))
        copies[-1].start()
    return copies


def unpack_body(distances, other, *refs):
    lines, count = len(distances), 6
    pieces, outs = refs[:lines], refs[lines : lines + count]
    stages, held, sems = refs[lines + count : -2], refs[-2], refs[-1]
    value = in_order(distances, pieces, held)
    half = jnp.bitwise_xor(lax.axis_index("feat"), other)
    copies = place_half(half, value, outs[:4], stages[:4], sems)
    row = sum(stage.shape[0] * (stage.shape[1] // 128) for stage in stages[:4])
    biases = []
    for out, stage in zip(outs[4:], stages[4:]):
        for c in range(stage.shape[1] // 128):
            stage[:, c * 128 : (c + 1) * 128] = value[row : row + 1, :]
            row += 1
        biases.append(pltpu.make_async_copy(stage, out, sems.at[len(copies) + len(biases)]))

    @pl.when(half == 0)
    def _():
        for copy in biases:
            copy.start()
        for copy in biases:
            copy.wait()

    for copy in copies:
        copy.wait()


def unpack_rest_body(distances, other, *refs):
    lines, count = len(distances), 6
    unpack_body(distances, other, *refs[:lines], *refs[lines + count :])


def shards(
    features,
    labels,
    local_index,
    local_values,
    cross_src,
    cross_dst,
    cross_count,
    cross_values,
    w1_self,
    w1_near,
    bias_one,
    w2_self,
    w2_near,
    bias_two,
):
    tiles, fan, size, _ = local_values.shape
    rounds, slots = cross_src.shape[1], cross_src.shape[2]
    width_in = features.shape[1]
    hidden_width = w1_self.shape[1]
    classes = w2_self.shape[1]
    nodes = tiles * size
    total_bits = lax.axis_size(AXES).bit_length() - 1
    masks = [1 << (total_bits - 1 - colour) for colour in range(rounds)]
    blocks = features.reshape(tiles, size, width_in)
    edges = cross_values[0]
    bias_one_row = bias_one.reshape(1, hidden_width)
    bias_two_row = bias_two.reshape(1, classes)
    label_rows = labels.reshape(tiles, size)

    at = Table(tiles, fan, rounds, slots)

    reads = cross_src.transpose(1, 0, 2)
    partner_src = [swapped(reads, mask) for mask in masks]
    blocks = run(
        stage_body,
        [HBM],
        VMEM,
        struct(blocks.shape, BF16),
        [pltpu.SemaphoreType.DMA],
        [blocks],
        moved=2 * nodes * width_in * 2,
    )
    picks = run(
        functools.partial(pick_body, rounds),
        [VMEM] * rounds + [VMEM],
        [VMEM] * rounds,
        [struct((slots, size, width_in), BF16)] * rounds,
        [],
        [*partner_src, blocks],
        moved=2 * rounds * slots * size * width_in * 2,
    )
    arrived = [swapped(tile, mask) for tile, mask in zip(picks, masks)]

    table, near, own, features_t, values_t, edges_t = run(
        functools.partial(first_local_body, at, rounds),
        [SMEM] * (3 + rounds) + [VMEM] * 5,
        [SMEM] + [VMEM] * 5,
        [
            pltpu.SMEM((at.size,), jnp.int32),
            struct((tiles, size, width_in), F32),
            struct((tiles, size, hidden_width), F32),
            struct((width_in + 16, nodes), BF16),
            struct(local_values.shape, BF16),
            struct(edges.shape, BF16),
        ],
        [],
        [
            local_index.T, cross_dst.transpose(1, 0, 2), cross_count, *partner_src,
            blocks, local_values, edges, w1_self, bias_one_row,
        ],
        flops=2 * nodes * width_in * (fan * size + hidden_width),
        moved=8 * 2**20,
    )

    first_agg, hidden, message, *sends = run(
        functools.partial(first_body, at, rounds),
        [SMEM] + [VMEM] * (rounds + 5),
        [VMEM] * (3 + rounds),
        [
            struct((tiles, size, width_in), BF16),
            struct((tiles, size, hidden_width), BF16),
            struct((tiles, size, classes), BF16),
        ]
        + [struct((slots, size, classes), BF16)] * rounds,
        [pltpu.VMEM((tiles + 1, size, width_in), F32)],
        [table, *arrived, edges, near, own, w1_near, w2_near],
        flops=2 * nodes * width_in * (rounds * slots * size // tiles + hidden_width + classes),
        moved=8 * 2**20,
    )
    arrived = [swapped(tile, mask) for tile, mask in zip(sends, masks)]

    slope, near, target, first_agg_t, hidden_t = run(
        functools.partial(second_local_body, at),
        [SMEM] + [VMEM] * 9,
        [VMEM] * 5,
        [
            struct((tiles, size, hidden_width), F32),
            struct((tiles, size, classes), F32),
            struct((tiles, size, classes), F32),
            struct((width_in, nodes), BF16),
            struct((hidden_width, nodes), BF16),
        ],
        [],
        [table, label_rows, local_values, first_agg, own, hidden, message, w1_near, w2_self, bias_two_row],
        flops=2 * nodes * classes * (fan * size + 3 * hidden_width),
        moved=6 * 2**20,
    )

    scores, error, *sends = run(
        functools.partial(second_body, at, rounds),
        [SMEM] + [VMEM] * (rounds + 4),
        [VMEM] * (2 + rounds),
        [struct((tiles, size, classes), BF16), struct((tiles, size, classes), BF16)]
        + [struct((slots, size, classes), BF16)] * rounds,
        [pltpu.VMEM((tiles + 1, size, classes), F32)],
        [table, *arrived, edges, edges_t, near, target],
        flops=4 * rounds * slots * size * size * classes,
        moved=3 * 2**20,
    )
    arrived = [swapped(tile, mask) for tile, mask in zip(sends, masks)]

    logits, back, self_grad, grad_w2_self, grad_bias_two = run(
        functools.partial(back_local_body, at),
        [SMEM] + [VMEM] * 5,
        [VMEM] * 5,
        [
            struct((tiles, size, classes), BF16),
            struct((tiles, size, classes), F32),
            struct((tiles, size, hidden_width), F32),
            struct((hidden_width, classes), F32),
            struct((1, classes), F32),
        ],
        [],
        [table, values_t, scores, error, hidden_t, w2_self],
        flops=2 * nodes * classes * (fan * size + 2 * hidden_width),
        moved=4 * 2**20,
    )

    lines, columns = lax.axis_size("dom"), lax.axis_size("sub")
    lines, columns = lax.axis_size("dom"), lax.axis_size("sub")
    matrices = [(width_in, hidden_width)] * 2 + [(hidden_width, classes)] * 2
    rows = sum(deep * width // 256 for deep, width in matrices) + (hidden_width + classes) // 128
    piece = -(-rows // (lines * 8)) * 8
    half = (lines, piece, 128)
    hidden_grad, send, keep = run(
        functools.partial(back_body, at, rounds),
        [SMEM] + [VMEM] * (rounds + 9),
        [VMEM] * 3,
        [
            struct((tiles, size, hidden_width), BF16),
            struct(half, BF16),
            struct(half, F32),
        ],
        [
            pltpu.VMEM((tiles, size, classes), F32),
            pltpu.VMEM((nodes, classes), BF16),
            pltpu.VMEM((nodes, hidden_width), BF16),
            pltpu.VMEM((2, lines * piece, 128), F32),
        ],
        [
            table, *arrived, back, self_grad, slope, w2_near, features_t, first_agg_t,
            hidden_t, grad_w2_self, grad_bias_two,
        ],
        flops=2 * nodes * hidden_width * (2 * width_in + 2 * classes),
        moved=6 * 2**20,
    )

    arrived = swapped(send, 1)
    hidden_grad = run(
        leave_body, [VMEM], VMEM, struct(hidden_grad.shape, BF16), [],
        [hidden_grad], moved=4 * nodes * hidden_width,
    )
    arrived, hidden_grad = lax.optimization_barrier((arrived, hidden_grad))

    along = [distance * 2 * columns for distance in range(1, lines)]
    piece_struct = struct((piece, 128), BF16)
    own, *sends = run(
        spread_body, [VMEM] * 2, [VMEM] * lines,
        [struct((piece, 128), F32)] + [piece_struct] * (lines - 1), [],
        [keep, arrived], flops=lines * piece * 128, moved=lines * piece * 128 * 8,
    )
    arrived = [swapped(value, mask) for value, mask in zip(sends, along)]
    total = run(
        gather_body, [VMEM] * lines, VMEM, piece_struct, [],
        [own, *arrived], flops=lines * piece * 128, moved=lines * piece * 128 * 2,
    )
    turned = (columns.bit_length() - 1) % 2
    for bit in range(columns.bit_length() - 1):
        total = run(
            gather_body, [VMEM] * 2, VMEM, piece_struct, [],
            [swapped(total, 1), swapped(total, (2 << bit) | 1)], flops=piece * 128, moved=piece * 128 * 6,
        )
    distances = [0, *range(2, 0, -1), *range(3, lines)]
    pieces = [total, *(swapped(total, along[distance - 1]) for distance in distances[1:])]
    copies = [swapped(value, 1) for value in pieces]
    shapes = matrices + [(1, hidden_width), (1, classes)]
    outs = [struct(shape, F32) for shape in shapes]
    scratch = [pltpu.VMEM((deep // 2, width), F32) for deep, width in matrices]
    scratch += [pltpu.VMEM(shape, F32) for shape in shapes[len(matrices) :]]
    scratch += [pltpu.VMEM(half, F32), pltpu.SemaphoreType.DMA((len(shapes),))]
    halves = run(
        functools.partial(unpack_body, distances, turned),
        [VMEM] * lines,
        [HBM] * len(outs),
        outs,
        scratch,
        pieces,
        moved=lines * piece * 128 * 6,
    )
    g1_self, g1_near, g2_self, g2_near, g1_bias, g2_bias = run(
        functools.partial(unpack_rest_body, distances, 1 - turned),
        [VMEM] * lines + [HBM] * len(outs),
        [HBM] * len(outs),
        outs,
        scratch,
        [*copies, *halves],
        moved=lines * piece * 128 * 6,
        aliases={lines + n: n for n in range(len(outs))},
    )
    return (
        logits.reshape(nodes, classes),
        hidden_grad.reshape(nodes, hidden_width),
        g1_self,
        g1_near,
        g1_bias.reshape(hidden_width),
        g2_self,
        g2_near,
        g2_bias.reshape(classes),
    )


def solution(mesh):
    in_specs = (
        P(("grp", "dom", "sub", "feat"), None),
        P(("grp", "dom", "sub", "feat")),
        P(("grp", "dom", "sub", "feat"), None),
        P(("grp", "dom", "sub", "feat"), None, None, None),
        P(("grp", "dom", "sub", "feat"), None, None),
        P(("grp", "dom", "sub", "feat"), None, None),
        P(("grp", "dom", "sub", "feat"), None),
        P(("grp", "dom", "sub", "feat"), None, None, None, None),
        P(),
        P(),
        P(),
        P(),
        P(),
        P(),
    )
    out_specs = (
        P(("grp", "dom", "sub", "feat"), None),
        P(("grp", "dom", "sub", "feat"), None),
        P("grp", None),
        P("grp", None),
        P("grp"),
        P("grp", None),
        P("grp", None),
        P("grp"),
    )
    return jax.shard_map(shards, mesh=mesh, in_specs=in_specs, out_specs=out_specs, check_vma=False)
```
